32 devices in a mesh: row: 4 (over y, core), col: 8 (over z, x).
Axes of the slice: x: 2, y: 2, z: 4, core: 2. Of those that a mesh axis runs over, the one named last changes fastest.
Arguments:
- tokens: bfloat16 [256, 16384], P('row', 'col'), may hold values from -6 to 6
- out_grad: bfloat16 [256, 16384], P('row', 'col'), may hold values from -6 to 6
- gate_values: bfloat16 [4, 8, 56, 128, 128], P('row', 'col'), may hold values from -0.3125 to 0.3125
- gate_exps: int32 [4, 8, 56], P('row', 'col'), may hold values from -1 to 1
- up_values: bfloat16 [4, 8, 56, 128, 128], P('row', 'col'), may hold values from -0.3125 to 0.3125
- up_exps: int32 [4, 8, 56], P('row', 'col'), may hold values from -1 to 1
- gate_up_ids: int32 [4, 8, 56], P('row', 'col'), may hold values from 0 to 896, as said below
- down_values: bfloat16 [4, 8, 56, 128, 128], P('row', 'col'), may hold values from -0.25 to 0.25
- down_exps: int32 [4, 8, 56], P('row', 'col'), may hold values from -1 to 1
- down_ids: int32 [4, 8, 56], P('row', 'col'), may hold values from 0 to 896, as said below
Outputs:
- output: bfloat16 [256, 16384], P('row', 'col')
- input_grad: bfloat16 [256, 16384], P('row', 'col')
- gate_grad: bfloat16 [4, 8, 56, 128, 128], P('row', 'col')
- up_grad: bfloat16 [4, 8, 56, 128, 128], P('row', 'col')
- down_grad: bfloat16 [4, 8, 56, 128, 128], P('row', 'col')
The draws below stay inside these ranges and needn't reach their ends.
Inputs may be any that keep to these rules, and one draw needn't show every extreme that they name: `gate_up_ids`: for each device (first two indices) the live entries name distinct blocks below 896 and come first; the value 896 marks an empty slot; on some device all 56 slots are live. `down_ids`: as for gate_up_ids.
All inputs are finite; a program needn't handle non-finite values.
Results may differ from the reference program's by a relative error of at most 0.005.
Values may be sent and summed in bfloat16 or wider, within the bound.
A program may use at most 320 MiB of HBM per device.

```python
import jax
import jax.numpy as jnp
from jax import lax

D = 16384
FF_WIN = 28672
BLK = 128
SLOTS = 56
TOKENS = 256
LB = 896
N_ROW = 4
N_COL = 8


def block_list(key):
    count_key, busy_key, score_key = jax.random.split(key, 3)
    devices_all = N_ROW * N_COL
    counts = jax.random.randint(count_key, (devices_all,), SLOTS // 6, SLOTS // 2 + 1)
    busiest = jax.random.randint(busy_key, (), 0, devices_all)
    counts = jnp.where(jnp.arange(devices_all) == busiest, SLOTS, counts)
    scores = jax.random.randint(score_key, (devices_all, LB), 0, 1 << 20) * LB + jnp.arange(LB)[None, :]
    ordering = jnp.argsort(scores, axis=1, stable=True)[:, :SLOTS]
    live_slot = jnp.arange(SLOTS)[None, :] < counts[:, None]
    chosen = jnp.where(live_slot, ordering, LB)
    return chosen.reshape(N_ROW, N_COL, SLOTS).astype(jnp.int32)


def draw_gate_up_ids(key, part):
    return block_list(jax.random.fold_in(key, 11))


def draw_down_ids(key, part):
    return block_list(jax.random.fold_in(key, 23))


def plant(result, rng, least, high):
    longest = result.shape.index(max(result.shape))
    spots = []
    for shift in (0, 1):
        where = [jax.random.randint(jax.random.fold_in(rng, axis), (), 0, length) for axis, length in enumerate(result.shape)]
        where[longest] = (where[longest] + shift) % result.shape[longest]
        spots.append(tuple(where))
    return result.at[spots[0]].set(least).at[spots[1]].set(high)


def steps_of(rng, shape, cuts, low, top_value):
    level, own = 1.0, jax.random.fold_in(rng, 6)
    for axis_at, shards_of in cuts:
        steps = jnp.exp(jax.random.uniform(jax.random.fold_in(own, axis_at), (shards_of,), jnp.float32, low / len(cuts), top_value / len(cuts)))
        level = level * jnp.repeat(steps, shape[axis_at] // shards_of).reshape([-1 if axis == axis_at else 1 for axis in range(len(shape))])
    return level


def bell_draw(stream_key, dims, scale, limit, cuts=(), held_as=jnp.bfloat16):
    entries = scale * jax.random.normal(stream_key, dims, jnp.float32)
    if cuts:
        entries = entries * steps_of(stream_key, dims, cuts, -0.22, 0.18)
    return jnp.clip(entries, -limit, limit).astype(held_as)


def setup_inputs(seed: int = 0) -> dict:
    key_list = jax.random.split(jax.random.key(seed), 11)
    tokens = bell_draw(key_list[0], (TOKENS, D), 1.0, 6.0, ((0, 4), (1, 8)))
    out_grad = bell_draw(key_list[1], (TOKENS, D), 1.0, 6.0, ((0, 4), (1, 8)))
    gate_values = bell_draw(key_list[2], (N_ROW, N_COL, SLOTS, BLK, BLK), (D * SLOTS // (3 * LB)) ** -0.5, 0.3125, ((0, 4), (1, 8)))
    gate_exps = plant(jax.random.randint(key_list[3], (N_ROW, N_COL, SLOTS), -1, 2), jax.random.fold_in(key_list[3], 1), -1, 1).astype(jnp.int32)
    up_values = bell_draw(key_list[4], (N_ROW, N_COL, SLOTS, BLK, BLK), (D * SLOTS // (3 * LB)) ** -0.5, 0.3125, ((0, 4), (1, 8)))
    up_exps = plant(jax.random.randint(key_list[5], (N_ROW, N_COL, SLOTS), -1, 2), jax.random.fold_in(key_list[5], 1), -1, 1).astype(jnp.int32)
    gate_up_ids = draw_gate_up_ids(jax.random.fold_in(key_list[10], 71), 0)
    down_values = bell_draw(key_list[7], (N_ROW, N_COL, SLOTS, BLK, BLK), (FF_WIN * SLOTS // (3 * LB)) ** -0.5, 0.25, ((0, 4), (1, 8)))
    down_exps = plant(jax.random.randint(key_list[8], (N_ROW, N_COL, SLOTS), -1, 2), jax.random.fold_in(key_list[8], 1), -1, 1).astype(jnp.int32)
    down_ids = draw_down_ids(jax.random.fold_in(key_list[10], 71), 0)
    return dict(tokens=tokens, out_grad=out_grad, gate_values=gate_values, gate_exps=gate_exps, up_values=up_values, up_exps=up_exps, gate_up_ids=gate_up_ids, down_values=down_values, down_exps=down_exps, down_ids=down_ids)


def exponent_scale(exponents):
    return jnp.where(exponents < 0, 0.5, jnp.where(exponents > 0, 2.0, 1.0)).astype(jnp.float32)


def place_column(values, exponents, block_ids, column):
    slot_values = values[:, column]
    slot_scales = exponent_scale(exponents[:, column])
    slot_ids = block_ids[:, column]
    scaled = (slot_values.astype(jnp.float32) * slot_scales[:, :, None, None]).astype(jnp.bfloat16)
    blank = jnp.zeros((LB + 1, BLK, BLK), jnp.bfloat16)

    def one_device(device_values, device_ids):
        return blank.at[device_ids].set(device_values)[:LB]

    return jax.vmap(one_device)(scaled, slot_ids)


def gate_like(values, exponents, block_ids, column):
    placed = place_column(values, exponents, block_ids, column)
    out_blocks = FF_WIN // (N_ROW * BLK)
    in_blocks = D // (N_COL * BLK)
    shaped = placed.reshape(N_ROW, out_blocks, in_blocks, BLK, BLK)
    return shaped.transpose(0, 1, 3, 2, 4).reshape(FF_WIN, D // N_COL)


def down_like(values, exponents, block_ids, column):
    placed = place_column(values, exponents, block_ids, column)
    out_blocks = D // (N_COL * BLK)
    in_blocks = FF_WIN // (N_ROW * BLK)
    shaped = placed.reshape(N_ROW, out_blocks, in_blocks, BLK, BLK)
    return shaped.transpose(1, 3, 0, 2, 4).reshape(D // N_COL, FF_WIN)


def pick_slots(dense_grad, block_ids, exponents, column, order):
    extended = jnp.concatenate([dense_grad, jnp.zeros((N_ROW, 1, BLK, BLK), dense_grad.dtype)], axis=1)
    slot_ids = block_ids[:, column].astype(jnp.int32)
    picked = jnp.take_along_axis(extended, slot_ids[:, :, None, None], axis=1)
    scales = exponent_scale(exponents[:, column])
    return (picked * scales[:, :, None, None]).astype(jnp.bfloat16)


def reference(tokens, out_grad, gate_values, gate_exps, up_values, up_exps, gate_up_ids, down_values, down_exps, down_ids):
    width = D // N_COL
    token_count = tokens.shape[0]
    columns = jnp.arange(N_COL, dtype=jnp.int32)

    def column_slice(array, column):
        return lax.dynamic_slice_in_dim(array, column * width, width, 1)

    def add_forward(carry, column):
        gate_acc, up_acc = carry
        token_cols = column_slice(tokens, column)
        gate_mat = gate_like(gate_values, gate_exps, gate_up_ids, column)
        up_mat = gate_like(up_values, up_exps, gate_up_ids, column)
        gate_part = jnp.dot(token_cols, gate_mat.T, preferred_element_type=jnp.float32)
        up_part = jnp.dot(token_cols, up_mat.T, preferred_element_type=jnp.float32)
        return (gate_acc + gate_part, up_acc + up_part), None

    zeros_hidden = jnp.zeros((token_count, FF_WIN), jnp.float32)
    (gate_sum, up_sum), _ = lax.scan(add_forward, (zeros_hidden, zeros_hidden), columns)
    hidden = (jax.nn.silu(gate_sum) * up_sum).astype(jnp.bfloat16)

    def output_column(column):
        down_mat = down_like(down_values, down_exps, down_ids, column)
        return jnp.dot(hidden, down_mat.T, preferred_element_type=jnp.float32).astype(jnp.bfloat16)

    output = lax.map(output_column, columns).transpose(1, 0, 2).reshape(token_count, D)

    def add_backward(carry, column):
        down_mat = down_like(down_values, down_exps, down_ids, column)
        grad_cols = column_slice(out_grad, column)
        partial_grad = jnp.dot(grad_cols, down_mat, preferred_element_type=jnp.float32)
        return carry + partial_grad, None

    hidden_grad, _ = lax.scan(add_backward, zeros_hidden, columns)
    sigmoid_gate = jax.nn.sigmoid(gate_sum)
    gate_act_grad = (hidden_grad * up_sum * sigmoid_gate * (1.0 + gate_sum * (1.0 - sigmoid_gate))).astype(jnp.bfloat16)
    up_act_grad = (hidden_grad * jax.nn.silu(gate_sum)).astype(jnp.bfloat16)

    def input_column(column):
        gate_mat = gate_like(gate_values, gate_exps, gate_up_ids, column)
        up_mat = gate_like(up_values, up_exps, gate_up_ids, column)
        summed = jnp.dot(gate_act_grad, gate_mat, preferred_element_type=jnp.float32)
        summed = summed + jnp.dot(up_act_grad, up_mat, preferred_element_type=jnp.float32)
        return summed.astype(jnp.bfloat16)

    input_grad = lax.map(input_column, columns).transpose(1, 0, 2).reshape(token_count, D)
    out_blocks = FF_WIN // (N_ROW * BLK)
    in_blocks = width // BLK

    def gate_up_column(column):
        token_cols = column_slice(tokens, column)
        gate_dense = jnp.dot(gate_act_grad.T, token_cols, preferred_element_type=jnp.float32)
        up_dense = jnp.dot(up_act_grad.T, token_cols, preferred_element_type=jnp.float32)

        def to_blocks(dense):
            shaped = dense.reshape(N_ROW, out_blocks, BLK, in_blocks, BLK).transpose(0, 1, 3, 2, 4)
            return shaped.reshape(N_ROW, LB, BLK, BLK)

        return (pick_slots(to_blocks(gate_dense), gate_up_ids, gate_exps, column, 0),
                pick_slots(to_blocks(up_dense), gate_up_ids, up_exps, column, 0))

    gate_stack, up_stack = lax.map(gate_up_column, columns)

    def down_column(column):
        grad_cols = column_slice(out_grad, column)
        dense = jnp.dot(grad_cols.T, hidden, preferred_element_type=jnp.float32)
        shaped = dense.reshape(in_blocks, BLK, N_ROW, out_blocks, BLK).transpose(2, 0, 3, 1, 4)
        return pick_slots(shaped.reshape(N_ROW, LB, BLK, BLK), down_ids, down_exps, column, 1)

    down_stack = lax.map(down_column, columns)
    gate_grad = gate_stack.transpose(1, 0, 2, 3, 4)
    up_grad = up_stack.transpose(1, 0, 2, 3, 4)
    down_grad = down_stack.transpose(1, 0, 2, 3, 4)
    return output, input_grad, gate_grad, up_grad, down_grad
```

```python
import functools

import jax
import jax.numpy as jnp
from jax import lax
from jax.experimental import pallas as pl
from jax.experimental.pallas import tpu as pltpu
from jax.sharding import PartitionSpec as P

FF_WIN = 28672
VMEM = pltpu.VMEM
SMEM = pltpu.SMEM


def scale_of(exponent):
    return jnp.where(exponent < 0, 0.5, jnp.where(exponent > 0, 2.0, 1.0)).astype(jnp.float32)


def scaled_block(values_ref, exps_ref, slot):
    scaled = values_ref[slot].astype(jnp.float32) * scale_of(exps_ref[slot])
    return scaled.astype(jnp.bfloat16)


def dot_nt(left, right):
    return lax.dot_general(left, right, (((1,), (1,)), ((), ())), preferred_element_type=jnp.float32)


def dot_nn(left, right):
    return lax.dot_general(left, right, (((1,), (0,)), ((), ())), preferred_element_type=jnp.float32)


def dot_tn(left, right):
    return lax.dot_general(left, right, (((0,), (0,)), ((), ())), preferred_element_type=jnp.float32)


def partial_kernel(
    pair_ids, down_ids, gate_exps, up_exps, down_exps,
    tokens, grads, gate_values, up_values, down_values,
    out, acc,
):
    slots, blk = gate_values.shape[0], gate_values.shape[1]
    width_blocks = tokens.shape[1] // blk
    hidden_blocks = acc.shape[0]
    count = hidden_blocks * width_blocks

    @pl.loop(0, hidden_blocks)
    def _(i):
        acc[i] = jnp.zeros(acc.shape[1:], jnp.float32)

    @pl.loop(0, slots)
    def _(s):
        pair = pair_ids[s]
        down = down_ids[s]

        @pl.when(pair < count)
        def _():
            i = pair // width_blocks
            j = pair % width_blocks
            cols = tokens[:, pl.ds(pl.multiple_of(j * blk, blk), blk)]
            weights = jnp.concatenate(
                [scaled_block(gate_values, gate_exps, s), scaled_block(up_values, up_exps, s)], axis=0
            )
            both = dot_nt(cols, weights)
            acc[i, 0] += both[:, :blk]
            acc[i, 1] += both[:, blk:]

        @pl.when(down < count)
        def _():
            i = down // hidden_blocks
            j = down % hidden_blocks
            cols = grads[:, pl.ds(pl.multiple_of(i * blk, blk), blk)]
            acc[j, 2] += dot_nn(cols, scaled_block(down_values, down_exps, s))

    @pl.loop(0, hidden_blocks)
    def _(i):
        out[i] = acc[i].astype(out.dtype)


def finish_kernel(
    pair_ids, down_ids, gate_exps, up_exps, down_exps,
    tokens, grads, gate_values, up_values, down_values, acts,
    parts, gate_grad, up_grad, down_grad,
):
    slots, blk = gate_values.shape[0], gate_values.shape[1]
    width_blocks = tokens.shape[1] // blk
    hidden_blocks = acts.shape[0]
    count = hidden_blocks * width_blocks

    parts[...] = jnp.zeros_like(parts)

    @pl.loop(0, slots)
    def _(s):
        pair = pair_ids[s]
        down = down_ids[s]

        @pl.when(pair < count)
        def _():
            i = pair // width_blocks
            j = pair % width_blocks
            at = pl.ds(pl.multiple_of(j * blk, blk), blk)
            cols = tokens[:, at]
            acts_both = jnp.concatenate([acts[i, 1], acts[i, 2]], axis=1)
            weights = jnp.concatenate(
                [scaled_block(gate_values, gate_exps, s), scaled_block(up_values, up_exps, s)], axis=0
            )
            parts[1, :, at] += dot_nn(acts_both, weights)
            both = dot_tn(acts_both, cols)
            gate_grad[s] = (both[:blk] * scale_of(gate_exps[s])).astype(jnp.bfloat16)
            up_grad[s] = (both[blk:] * scale_of(up_exps[s])).astype(jnp.bfloat16)

        @pl.when(pair >= count)
        def _():
            gate_grad[s] = jnp.zeros((blk, blk), jnp.bfloat16)
            up_grad[s] = jnp.zeros((blk, blk), jnp.bfloat16)

        @pl.when(down < count)
        def _():
            i = down // hidden_blocks
            j = down % hidden_blocks
            at = pl.ds(pl.multiple_of(i * blk, blk), blk)
            hidden = acts[j, 0]
            parts[0, :, at] += dot_nt(hidden, scaled_block(down_values, down_exps, s))
            grad = dot_tn(grads[:, at], hidden)
            down_grad[s] = (grad * scale_of(down_exps[s])).astype(jnp.bfloat16)

        @pl.when(down >= count)
        def _():
            down_grad[s] = jnp.zeros((blk, blk), jnp.bfloat16)


def derive(gate_sum, up_sum, hidden_grad):
    sigmoid_gate = jax.nn.sigmoid(gate_sum)
    silu = gate_sum * sigmoid_gate
    hidden = silu * up_sum
    gate_piece = hidden_grad * up_sum * sigmoid_gate * (1.0 + gate_sum * (1.0 - sigmoid_gate))
    up_piece = hidden_grad * silu
    return hidden, gate_piece, up_piece


def exchange_xla(partial):
    summed = lax.psum_scatter(partial, "col", scatter_dimension=2, tiled=True).astype(jnp.float32)
    acts = jnp.stack(derive(summed[:, 0], summed[:, 1], summed[:, 2]), axis=1).astype(jnp.bfloat16)
    return lax.all_gather(acts, "col", axis=2, tiled=True)


def activations(sums):
    return [part.astype(jnp.bfloat16) for part in derive(*sums)]


def exchange_kernel(
    n_z, step_blocks, ahead,
    partial, acts,
    own, from_x, from_left, from_right, to_left, to_right, stage,
    own_sem, x_send, x_recv, right_send, right_recv, left_send, left_recv, act_send, act_recv, keep_sem,
):
    col = lax.axis_index("col")
    z, x = col // 2, col % 2
    peer, right, left = z * 2 + (1 - x), col + 2, col - 2
    half = partial.shape[2] // 2
    steps = partial.shape[0] // step_blocks
    lag = n_z
    mine = pl.ds(pl.multiple_of(x * half, half), half)
    theirs = pl.ds(pl.multiple_of((1 - x) * half, half), half)

    def blocks(k):
        return pl.ds(k * step_blocks, step_blocks)

    def remote(src, dst, send, recv, target):
        return pltpu.make_async_remote_copy(
            src_ref=src, dst_ref=dst, send_sem=send, recv_sem=recv,
            device_id={"col": target}, device_id_type=pl.DeviceIdType.MESH,
        )

    def x_copy(k):
        return remote(partial.at[blocks(k), :, theirs], from_x.at[blocks(k)], x_send.at[k], x_recv.at[k], peer)

    def right_copy(k):
        return remote(to_right.at[blocks(k)], from_left.at[blocks(k)], right_send.at[k], right_recv.at[k], right)

    def left_copy(k):
        return remote(to_left.at[blocks(k)], from_right.at[blocks(k)], left_send.at[k], left_recv.at[k], left)

    def act_copy(k):
        return remote(stage.at[blocks(k)], acts.at[blocks(k), :, mine], act_send.at[k], act_recv.at[k], peer)

    def keep_copy(k):
        return pltpu.make_async_copy(stage.at[blocks(k)], acts.at[blocks(k), :, mine], keep_sem.at[k])

    barrier = pltpu.get_barrier_semaphore()

    def greet(target):
        pl.semaphore_signal(barrier, inc=1, device_id={"col": target}, device_id_type=pl.DeviceIdType.MESH)

    greet(peer)
    pl.when(z > 0)(lambda: greet(left))
    pl.when(z < n_z - 1)(lambda: greet(right))
    pl.semaphore_wait(barrier, 1 + (z > 0).astype(jnp.int32) + (z < n_z - 1).astype(jnp.int32))

    own_copy = pltpu.make_async_copy(partial.at[:, :, mine], own, own_sem)
    own_copy.start()
    for k in range(ahead):
        x_copy(k).start()
    own_copy.wait()

    def each_block(k, body):
        @pl.loop(0, step_blocks)
        def _(b):
            body(k * step_blocks + b)

    def add_pair(i):
        for u in range(3):
            total = own[i, u].astype(jnp.float32) + from_x[i, u].astype(jnp.float32)
            own[i, u] = total.astype(jnp.bfloat16)

    def forward(source, target):
        def body(i):
            for u in range(3):
                total = own[i, u].astype(jnp.float32) + source[i, u].astype(jnp.float32)
                target[i, u] = total.astype(jnp.bfloat16)
        return body

    def start_chain(target):
        def body(i):
            target[i] = own[i]
        return body

    def finish(sources):
        def body(i):
            sums = []
            for u in range(3):
                total = own[i, u].astype(jnp.float32)
                for source in sources:
                    total += source[i, u].astype(jnp.float32)
                sums.append(total)
            for u, part in enumerate(activations(sums)):
                stage[i, u] = part
        return body

    @pl.loop(0, steps + lag)
    def _(t):
        @pl.when(t + ahead < steps)
        def _():
            x_copy(t + ahead).start()

        @pl.when(t < steps)
        def _():
            x_copy(t).wait_recv()
            each_block(t, add_pair)

        r = t - z

        @pl.when((r >= 0) & (r < steps) & (z < n_z - 1))
        def _():
            @pl.when(z == 0)
            def _():
                each_block(r, start_chain(to_right))

            @pl.when(z > 0)
            def _():
                right_copy(r).wait_recv()
                each_block(r, forward(from_left, to_right))

            right_copy(r).start()

        l = t - (n_z - 1 - z)

        @pl.when((l >= 0) & (l < steps) & (z > 0))
        def _():
            @pl.when(z == n_z - 1)
            def _():
                each_block(l, start_chain(to_left))

            @pl.when(z < n_z - 1)
            def _():
                left_copy(l).wait_recv()
                each_block(l, forward(from_right, to_left))

            left_copy(l).start()

        f = t - lag

        @pl.when(f >= 0)
        def _():
            @pl.when(z == 0)
            def _():
                left_copy(f).wait_recv()
                each_block(f, finish([from_right]))

            @pl.when(z == n_z - 1)
            def _():
                right_copy(f).wait_recv()
                each_block(f, finish([from_left]))

            @pl.when((z > 0) & (z < n_z - 1))
            def _():
                each_block(f, finish([from_left, from_right]))

            act_copy(f).start()
            keep_copy(f).start()

    @pl.loop(0, steps)
    def _(k):
        x_copy(k).wait_send()
        pl.when(z < n_z - 1)(lambda: right_copy(k).wait_send())
        pl.when(z > 0)(lambda: left_copy(k).wait_send())
        act_copy(k).wait()
        keep_copy(k).wait()


def exchange(partial, n_col):
    blocks, units, total, blk = partial.shape
    step_blocks = 2
    steps = blocks // step_blocks
    buffer = pltpu.VMEM((blocks, units, total // 2, blk), jnp.bfloat16)
    sems = pltpu.SemaphoreType.DMA((steps,))
    return pl.pallas_call(
        functools.partial(exchange_kernel, n_col // 2, step_blocks, min(6, steps)),
        out_shape=jax.ShapeDtypeStruct(partial.shape, jnp.bfloat16),
        in_specs=[pl.BlockSpec(memory_space=pl.ANY)],
        out_specs=pl.BlockSpec(memory_space=pl.ANY),
        scratch_shapes=[buffer] * 7 + [pltpu.SemaphoreType.DMA(())] + [sems] * 9,
        compiler_params=pltpu.CompilerParams(
            collective_id=0, has_side_effects=True, vmem_limit_bytes=60 * 1024 * 1024
        ),
        name="exchange",
    )(partial)


def on_device(
    n_row, n_col,
    tokens, out_grad, gate_values, gate_exps, up_values, up_exps, gate_up_ids,
    down_values, down_exps, down_ids,
):
    blk = gate_values.shape[-1]
    slots = gate_values.shape[2]
    pair_slots, down_slots = gate_up_ids[0, 0], down_ids[0, 0]
    exps = (gate_exps[0, 0], up_exps[0, 0], down_exps[0, 0])
    values = (gate_values[0, 0], up_values[0, 0], down_values[0, 0])
    tokens_all = lax.all_gather(tokens, "row", axis=0, tiled=True)
    grads_all = lax.all_gather(out_grad, "row", axis=0, tiled=True)
    total, width = tokens_all.shape
    hidden_blocks = FF_WIN // n_row // blk
    smem = pl.BlockSpec(memory_space=SMEM)
    vmem = pl.BlockSpec(memory_space=VMEM)
    params = pltpu.CompilerParams(vmem_limit_bytes=60 * 1024 * 1024)
    partial = pl.pallas_call(
        partial_kernel,
        out_shape=jax.ShapeDtypeStruct((hidden_blocks, 3, total, blk), jnp.bfloat16),
        in_specs=[smem] * 5 + [vmem] * 5,
        out_specs=vmem,
        scratch_shapes=[pltpu.VMEM((hidden_blocks, 3, total, blk), jnp.float32)],
        compiler_params=params,
        name="partial_sums",
    )(pair_slots, down_slots, *exps, tokens_all, grads_all, *values)
    paired = (n_row, n_col) == (4, 8)
    acts = exchange(partial, n_col) if paired else exchange_xla(partial)
    grad_shape = jax.ShapeDtypeStruct((slots, blk, blk), jnp.bfloat16)
    parts, gate_grad, up_grad, down_grad = pl.pallas_call(
        finish_kernel,
        out_shape=(jax.ShapeDtypeStruct((2, total, width), jnp.float32), grad_shape, grad_shape, grad_shape),
        in_specs=[smem] * 5 + [vmem] * 6,
        out_specs=(vmem,) * 4,
        compiler_params=params,
        name="finish",
    )(pair_slots, down_slots, *exps, tokens_all, grads_all, *values, acts)
    rows = lax.psum_scatter(parts, "row", scatter_dimension=1, tiled=True)
    rows = rows.astype(jnp.bfloat16)
    return rows[0], rows[1], gate_grad[None, None], up_grad[None, None], down_grad[None, None]


def solution(mesh):
    lists = P("row", "col", None, None, None)
    ids = P("row", "col", None)
    in_specs = (P("row", "col"), P("row", "col"), lists, ids, lists, ids, ids, lists, ids, ids)
    out_specs = (P("row", "col"), P("row", "col"), lists, lists, lists)
    body = functools.partial(on_device, mesh.shape["row"], mesh.shape["col"])
    return jax.shard_map(body, mesh=mesh, in_specs=in_specs, out_specs=out_specs, check_vma=False)
```

```python
import functools

import jax
import jax.numpy as jnp
from jax import lax
from jax.experimental import pallas as pl
from jax.experimental.pallas import tpu as pltpu
from jax.sharding import PartitionSpec as P

FF_WIN = 28672
VMEM = pltpu.VMEM
SMEM = pltpu.SMEM


def scale_of(exponent):
    return jnp.where(exponent < 0, 0.5, jnp.where(exponent > 0, 2.0, 1.0)).astype(jnp.float32)


def scaled_block(values_ref, exps_ref, slot):
    scaled = values_ref[slot].astype(jnp.float32) * scale_of(exps_ref[slot])
    return scaled.astype(jnp.bfloat16)


def dot_nt(left, right):
    return lax.dot_general(left, right, (((1,), (1,)), ((), ())), preferred_element_type=jnp.float32)


def dot_nn(left, right):
    return lax.dot_general(left, right, (((1,), (0,)), ((), ())), preferred_element_type=jnp.float32)


def dot_tn(left, right):
    return lax.dot_general(left, right, (((0,), (0,)), ((), ())), preferred_element_type=jnp.float32)


def partial_kernel(
    pair_ids, down_ids, gate_exps, up_exps, down_exps,
    tokens, grads, gate_values, up_values, down_values,
    *rest,
):
    acc = rest[-1]
    slots, blk = gate_values.shape[0], gate_values.shape[1]
    width_blocks = tokens.shape[1] // blk
    hidden_blocks = acc.shape[0]
    count = hidden_blocks * width_blocks

    @pl.loop(0, hidden_blocks)
    def _(i):
        acc[i] = jnp.zeros(acc.shape[1:], jnp.float32)

    @pl.loop(0, slots)
    def _(s):
        pair = pair_ids[s]
        down = down_ids[s]

        @pl.when(pair < count)
        def _():
            i = pair // width_blocks
            j = pair % width_blocks
            cols = tokens[:, pl.ds(pl.multiple_of(j * blk, blk), blk)]
            weights = jnp.concatenate(
                [scaled_block(gate_values, gate_exps, s), scaled_block(up_values, up_exps, s)], axis=0
            )
            both = dot_nt(cols, weights)
            acc[i, 0] += both[:, :blk]
            acc[i, 1] += both[:, blk:]

        @pl.when(down < count)
        def _():
            i = down // hidden_blocks
            j = down % hidden_blocks
            cols = grads[:, pl.ds(pl.multiple_of(i * blk, blk), blk)]
            acc[j, 2] += dot_nn(cols, scaled_block(down_values, down_exps, s))

    if len(rest) == 2:
        @pl.loop(0, hidden_blocks)
        def _(i):
            rest[0][i] = acc[i].astype(rest[0].dtype)
    else:
        sent, own, full = rest[:3]
        paired, half = own.shape[0], own.shape[2]
        x = lax.axis_index("col") % 2
        mine = pl.ds(pl.multiple_of(x * half, half), half)
        theirs = pl.ds(pl.multiple_of((1 - x) * half, half), half)

        @pl.loop(0, paired)
        def _(i):
            sent[i] = acc[i, :, theirs].astype(sent.dtype)
            own[i] = acc[i, :, mine]

        @pl.loop(paired, hidden_blocks)
        def _(i):
            full[i - paired] = acc[i]


def finish_kernel(
    pair_ids, down_ids, gate_exps, up_exps, down_exps,
    tokens, grads, gate_values, up_values, down_values, acts,
    parts, gate_grad, up_grad, down_grad,
):
    slots, blk = gate_values.shape[0], gate_values.shape[1]
    width_blocks = tokens.shape[1] // blk
    hidden_blocks = acts.shape[0]
    count = hidden_blocks * width_blocks

    parts[...] = jnp.zeros_like(parts)

    @pl.loop(0, slots)
    def _(s):
        pair = pair_ids[s]
        down = down_ids[s]

        @pl.when(pair < count)
        def _():
            i = pair // width_blocks
            j = pair % width_blocks
            at = pl.ds(pl.multiple_of(j * blk, blk), blk)
            cols = tokens[:, at]
            acts_both = jnp.concatenate([acts[i, 1], acts[i, 2]], axis=1)
            weights = jnp.concatenate(
                [scaled_block(gate_values, gate_exps, s), scaled_block(up_values, up_exps, s)], axis=0
            )
            parts[1, :, at] += dot_nn(acts_both, weights)
            both = dot_tn(acts_both, cols)
            gate_grad[s] = (both[:blk] * scale_of(gate_exps[s])).astype(jnp.bfloat16)
            up_grad[s] = (both[blk:] * scale_of(up_exps[s])).astype(jnp.bfloat16)

        @pl.when(pair >= count)
        def _():
            gate_grad[s] = jnp.zeros((blk, blk), jnp.bfloat16)
            up_grad[s] = jnp.zeros((blk, blk), jnp.bfloat16)

        @pl.when(down < count)
        def _():
            i = down // hidden_blocks
            j = down % hidden_blocks
            at = pl.ds(pl.multiple_of(i * blk, blk), blk)
            hidden = acts[j, 0]
            parts[0, :, at] += dot_nt(hidden, scaled_block(down_values, down_exps, s))
            grad = dot_tn(grads[:, at], hidden)
            down_grad[s] = (grad * scale_of(down_exps[s])).astype(jnp.bfloat16)

        @pl.when(down >= count)
        def _():
            down_grad[s] = jnp.zeros((blk, blk), jnp.bfloat16)


def derive(gate_sum, up_sum, hidden_grad):
    sigmoid_gate = jax.nn.sigmoid(gate_sum)
    silu = gate_sum * sigmoid_gate
    hidden = silu * up_sum
    gate_piece = hidden_grad * up_sum * sigmoid_gate * (1.0 + gate_sum * (1.0 - sigmoid_gate))
    up_piece = hidden_grad * silu
    return hidden, gate_piece, up_piece


def exchange_xla(partial):
    summed = lax.psum_scatter(partial, "col", scatter_dimension=2, tiled=True).astype(jnp.float32)
    acts = jnp.stack(derive(summed[:, 0], summed[:, 1], summed[:, 2]), axis=1).astype(jnp.bfloat16)
    return lax.all_gather(acts, "col", axis=2, tiled=True)


def activations(sums):
    return [part.astype(jnp.bfloat16) for part in derive(*sums)]


def exchange_kernel(
    n_z, ahead,
    sent, own_in, full_in, acts,
    own, from_x, from_left, from_right, to_left, to_right, stage,
    full, in_left, in_right, chain, pair_out, pair_in, joined,
    load_sem, a_send, a_recv, b_send, b_recv, pair_send, pair_recv, keep_sem, out_sem,
):
    col = lax.axis_index("col")
    z, x = col // 2, col % 2
    peer, right, left = z * 2 + (1 - x), col + 2, col - 2
    last = n_z - 1
    half = own.shape[2]
    quarter = full.shape[2] // n_z
    n_a, n_b = own.shape[0], full.shape[0]
    mine = pl.ds(pl.multiple_of(x * half, half), half)
    my_quarter = pl.ds(pl.multiple_of(z * quarter, quarter), quarter)

    def rows(d):
        return pl.ds(d * quarter, quarter)

    def remote(src, dst, send, recv, target):
        return pltpu.make_async_remote_copy(
            src_ref=src, dst_ref=dst, send_sem=send, recv_sem=recv,
            device_id={"col": target}, device_id_type=pl.DeviceIdType.MESH,
        )

    def x_copy(k):
        return remote(sent.at[k], from_x.at[k], a_send.at[0, k], a_recv.at[0, k], peer)

    def right_copy(k):
        return remote(to_right.at[k], from_left.at[k], a_send.at[1, k], a_recv.at[1, k], right)

    def left_copy(k):
        return remote(to_left.at[k], from_right.at[k], a_send.at[2, k], a_recv.at[2, k], left)

    def act_copy(k):
        return remote(stage.at[k], acts.at[k, :, mine], a_send.at[3, k], a_recv.at[3, k], peer)

    def keep_copy(k):
        return pltpu.make_async_copy(stage.at[k], acts.at[k, :, mine], keep_sem.at[k])

    def chain_right(k, d):
        return remote(chain.at[k, :, rows(d)], in_left.at[k, :, rows(d)], b_send.at[0, d, k], b_recv.at[0, d, k], right)

    def chain_left(k, d):
        return remote(chain.at[k, :, rows(d)], in_right.at[k, :, rows(d)], b_send.at[1, d, k], b_recv.at[1, d, k], left)

    def pair_copy(k):
        return remote(pair_out.at[k], pair_in.at[k], pair_send.at[k], pair_recv.at[k], peer)

    def gather_right(k, d):
        return remote(joined.at[k, :, rows(d)], joined.at[k, :, rows(d)], b_send.at[2, d, k], b_recv.at[2, d, k], right)

    def gather_left(k, d):
        return remote(joined.at[k, :, rows(d)], joined.at[k, :, rows(d)], b_send.at[3, d, k], b_recv.at[3, d, k], left)

    def out_copy(k):
        return pltpu.make_async_copy(joined.at[k], acts.at[n_a + k], out_sem.at[k])

    barrier = pltpu.get_barrier_semaphore()

    def greet(target):
        pl.semaphore_signal(barrier, inc=1, device_id={"col": target}, device_id_type=pl.DeviceIdType.MESH)

    greet(peer)
    pl.when(z > 0)(lambda: greet(left))
    pl.when(z < last)(lambda: greet(right))
    pl.semaphore_wait(barrier, 1 + (z > 0).astype(jnp.int32) + (z < last).astype(jnp.int32))

    own_load = pltpu.make_async_copy(own_in, own, load_sem.at[0])
    full_load = pltpu.make_async_copy(full_in, full, load_sem.at[1])
    for k in range(min(ahead, n_a)):
        x_copy(k).start()
    full_load.start()
    own_load.start()
    full_load.wait()
    own_load.wait()

    def f32(value):
        return value.astype(jnp.float32)

    def join(k, target, sources):
        for u in range(3):
            total = own[k, u]
            for source in sources:
                total += f32(source[k, u])
            target[k, u] = total.astype(target.dtype)

    def finish(k, sources):
        sums = []
        for u in range(3):
            total = own[k, u]
            for source in sources:
                total += f32(source[k, u])
            sums.append(total)
        for u, part in enumerate(activations(sums)):
            stage[k, u] = part

    def paired_step(t):
        @pl.when(t < n_a)
        def _():
            x_copy(t).wait_recv()
            join(t, own, [from_x])

        r = t - z

        @pl.when((r >= 0) & (r < n_a) & (z < last))
        def _():
            @pl.when(z == 0)
            def _():
                join(r, to_right, [])

            @pl.when(z > 0)
            def _():
                right_copy(r).wait_recv()
                join(r, to_right, [from_left])

            right_copy(r).start()

        l = t - (last - z)

        @pl.when((l >= 0) & (l < n_a) & (z > 0))
        def _():
            @pl.when(z == last)
            def _():
                join(l, to_left, [])

            @pl.when(z < last)
            def _():
                left_copy(l).wait_recv()
                join(l, to_left, [from_right])

            left_copy(l).start()

        f = t - n_z

        @pl.when((f >= 0) & (f < n_a))
        def _():
            @pl.when(z == 0)
            def _():
                left_copy(f).wait_recv()
                finish(f, [from_right])

            @pl.when(z == last)
            def _():
                right_copy(f).wait_recv()
                finish(f, [from_left])

            @pl.when((z > 0) & (z < last))
            def _():
                finish(f, [from_left, from_right])

            act_copy(f).start()
            keep_copy(f).start()

    def join_rows(k, d, sources):
        for u in range(3):
            total = full[k, u, rows(d)]
            for source in sources:
                total += f32(source[k, u, rows(d)])
            chain[k, u, rows(d)] = total.astype(chain.dtype)

    def chain_step(t):
        r = t - z

        @pl.when((r >= 0) & (r < n_b))
        def _():
            for d in range(1, n_z):
                @pl.when(d > z)
                def _():
                    @pl.when(z == 0)
                    def _():
                        join_rows(r, d, [])

                    @pl.when(z > 0)
                    def _():
                        chain_right(r, d).wait_recv()
                        join_rows(r, d, [in_left])

                    chain_right(r, d).start()

        l = t - (last - z)

        @pl.when((l >= 0) & (l < n_b))
        def _():
            for d in range(last):
                @pl.when(d < z)
                def _():
                    @pl.when(z == last)
                    def _():
                        join_rows(l, d, [])

                    @pl.when(z < last)
                    def _():
                        chain_left(l, d).wait_recv()
                        join_rows(l, d, [in_right])

                    chain_left(l, d).start()

        f = t - n_z

        @pl.when((f >= 0) & (f < n_b))
        def _():
            def add_mine(source):
                for u in range(3):
                    full[f, u, my_quarter] += f32(source[f, u, my_quarter])

            @pl.when(z > 0)
            def _():
                chain_right(f, z).wait_recv()
                add_mine(in_left)

            @pl.when(z < last)
            def _():
                chain_left(f, z).wait_recv()
                add_mine(in_right)

            pair_out[f] = full[f, :, my_quarter].astype(pair_out.dtype)
            pair_copy(f).start()

        g = t - n_z - 2

        @pl.when((g >= 0) & (g < n_b))
        def _():
            pair_copy(g).wait_recv()
            sums = [full[g, u, my_quarter] + f32(pair_in[g, u]) for u in range(3)]
            for u, part in enumerate(activations(sums)):
                joined[g, u, my_quarter] = part
            pl.when(z < last)(lambda: gather_right(g, z).start())
            pl.when(z > 0)(lambda: gather_left(g, z).start())

        for d in range(n_z):
            right_at = g - (z - d)
            left_at = g - (d - z)

            @pl.when((d < z) & (right_at >= 0) & (right_at < n_b))
            def _():
                gather_right(right_at, d).wait_recv()
                pl.when(z < last)(lambda: gather_right(right_at, d).start())

            @pl.when((d > z) & (left_at >= 0) & (left_at < n_b))
            def _():
                gather_left(left_at, d).wait_recv()
                pl.when(z > 0)(lambda: gather_left(left_at, d).start())

        done = g - last

        @pl.when((done >= 0) & (done < n_b))
        def _():
            out_copy(done).start()

    @pl.loop(0, max(n_a + n_z, n_b + n_z + 2 + last) + 1)
    def _(t):
        first = ahead + t + (t + 1) // 2

        @pl.when(first < n_a)
        def _():
            x_copy(first).start()

        @pl.when((t % 2 == 0) & (first + 1 < n_a))
        def _():
            x_copy(first + 1).start()

        chain_step(t)
        paired_step(t)

    @pl.loop(0, n_a)
    def _(k):
        x_copy(k).wait_send()
        pl.when(z < last)(lambda: right_copy(k).wait_send())
        pl.when(z > 0)(lambda: left_copy(k).wait_send())
        act_copy(k).wait()
        keep_copy(k).wait()

    @pl.loop(0, n_b)
    def _(k):
        pair_copy(k).wait_send()
        out_copy(k).wait()
        for d in range(n_z):
            pl.when(d > z)(lambda: chain_right(k, d).wait_send())
            pl.when(d < z)(lambda: chain_left(k, d).wait_send())
            pl.when((d <= z) & (z < last))(lambda: gather_right(k, d).wait_send())
            pl.when((d >= z) & (z > 0))(lambda: gather_left(k, d).wait_send())


def exchange(sent, own, full, n_col):
    n_a, units, half, blk = own.shape
    n_b, total = full.shape[0], full.shape[2]
    n_z = n_col // 2
    bf16 = jnp.bfloat16
    halves = pltpu.VMEM((n_a, units, half, blk), bf16)
    wholes = pltpu.VMEM((n_b, units, total, blk), bf16)
    quarters = pltpu.VMEM((n_b, units, total // n_z, blk), bf16)
    dma = pltpu.SemaphoreType.DMA
    anywhere = pl.BlockSpec(memory_space=pl.ANY)
    return pl.pallas_call(
        functools.partial(exchange_kernel, n_z, min(4, n_a)),
        out_shape=jax.ShapeDtypeStruct((n_a + n_b, units, total, blk), bf16),
        in_specs=[anywhere] * 3,
        out_specs=anywhere,
        scratch_shapes=[pltpu.VMEM(own.shape, jnp.float32)] + [halves] * 6
        + [pltpu.VMEM(full.shape, jnp.float32)] + [wholes] * 3 + [quarters] * 2 + [wholes]
        + [dma((2,)), dma((4, n_a)), dma((4, n_a)), dma((4, n_z, n_b)), dma((4, n_z, n_b))]
        + [dma((n_b,)), dma((n_b,)), dma((n_a,)), dma((n_b,))],
        compiler_params=pltpu.CompilerParams(
            collective_id=0, has_side_effects=True, vmem_limit_bytes=60 * 1024 * 1024
        ),
        name="exchange",
    )(sent, own, full)


def row_neighbours():
    row = lax.axis_index("row")
    y, core = row // 2, row % 2
    return row, y, core, (1 - y) * 2 + core, y * 2 + (1 - core)


def row_remote(src, dst, send, recv, target):
    return pltpu.make_async_remote_copy(
        src_ref=src, dst_ref=dst, send_sem=send, recv_sem=recv,
        device_id={"row": target}, device_id_type=pl.DeviceIdType.MESH,
    )


def row_barrier(targets):
    barrier = pltpu.get_barrier_semaphore()
    for target in targets:
        pl.semaphore_signal(barrier, inc=1, device_id={"row": target}, device_id_type=pl.DeviceIdType.MESH)
    pl.semaphore_wait(barrier, len(targets))


def gather_kernel(tokens, grads, tokens_all, grads_all, send, recv, keep):
    row, y, core, far, near = row_neighbours()
    share = tokens.shape[0]
    row_barrier((far, near))

    def rows(index):
        return pl.ds(pl.multiple_of(index * share, share), share)

    pairs = ((tokens, tokens_all), (grads, grads_all))
    across = [row_remote(src, dst.at[rows(row)], send.at[0, a], recv.at[0, a], far) for a, (src, dst) in enumerate(pairs)]
    beside = [row_remote(src, dst.at[rows(row)], send.at[1, a], recv.at[1, a], near) for a, (src, dst) in enumerate(pairs)]
    onward = [
        row_remote(dst.at[rows(far)], dst.at[rows(far)], send.at[2, a], recv.at[2, a], near)
        for a, (src, dst) in enumerate(pairs)
    ]
    local = [pltpu.make_async_copy(src, dst.at[rows(row)], keep.at[a]) for a, (src, dst) in enumerate(pairs)]
    for copy in across + beside + local:
        copy.start()
    for a in range(2):
        across[a].wait_recv()
        onward[a].start()
    for a in range(2):
        across[a].wait_send()
        beside[a].wait()
        onward[a].wait()
        local[a].wait()


def gather_rows(tokens, grads, n_row):
    whole = jax.ShapeDtypeStruct((tokens.shape[0] * n_row, tokens.shape[1]), tokens.dtype)
    anywhere = pl.BlockSpec(memory_space=pl.ANY)
    dma = pltpu.SemaphoreType.DMA
    return pl.pallas_call(
        gather_kernel,
        out_shape=(whole, whole),
        in_specs=[anywhere] * 2,
        out_specs=(anywhere,) * 2,
        scratch_shapes=[dma((3, 2)), dma((3, 2)), dma((2,))],
        compiler_params=pltpu.CompilerParams(collective_id=1, has_side_effects=True),
        name="gather_rows",
    )(tokens, grads)


def sum_kernel(parts, output, input_grad, from_near, to_far, from_far, send, recv):
    row, y, core, far, near = row_neighbours()
    share = output.shape[0]
    results = (output, input_grad)
    row_barrier((far, near))

    def rows(index):
        return pl.ds(pl.multiple_of(index * share, share), share)

    def near_copy(place, u):
        index = jnp.where(place == 0, 1 - y, y) * 2 + (1 - core)
        return row_remote(
            parts.at[u, rows(index)], from_near.at[place, u], send.at[place, u], recv.at[place, u], near
        )

    def far_copy(u):
        return row_remote(to_far.at[u], from_far.at[u], send.at[2, u], recv.at[2, u], far)

    for place in range(2):
        for u in range(2):
            near_copy(place, u).start()
    for u in range(2):
        near_copy(0, u).wait_recv()
        to_far[u] = (parts[u, rows(far)] + from_near[0, u]).astype(to_far.dtype)
        far_copy(u).start()
    for u in range(2):
        near_copy(1, u).wait_recv()
        from_near[1, u] += parts[u, rows(row)]
    for u in range(2):
        far_copy(u).wait_recv()
        results[u][...] = (from_near[1, u] + from_far[u].astype(jnp.float32)).astype(jnp.bfloat16)
    for u in range(2):
        near_copy(0, u).wait_send()
        near_copy(1, u).wait_send()
        far_copy(u).wait_send()


def sum_rows(parts, n_row):
    units, total, width = parts.shape
    share = total // n_row
    result = jax.ShapeDtypeStruct((share, width), jnp.bfloat16)
    vmem = pl.BlockSpec(memory_space=VMEM)
    dma = pltpu.SemaphoreType.DMA
    return pl.pallas_call(
        sum_kernel,
        out_shape=(result, result),
        in_specs=[vmem],
        out_specs=(vmem, vmem),
        scratch_shapes=[
            pltpu.VMEM((2, units, share, width), jnp.float32),
            pltpu.VMEM((units, share, width), jnp.bfloat16),
            pltpu.VMEM((units, share, width), jnp.bfloat16),
            dma((3, units)), dma((3, units)),
        ],
        compiler_params=pltpu.CompilerParams(
            collective_id=2, has_side_effects=True, vmem_limit_bytes=32 * 1024 * 1024
        ),
        name="sum_rows",
    )(parts)


def on_device(
    n_row, n_col,
    tokens, out_grad, gate_values, gate_exps, up_values, up_exps, gate_up_ids,
    down_values, down_exps, down_ids,
):
    blk = gate_values.shape[-1]
    slots = gate_values.shape[2]
    pair_slots, down_slots = gate_up_ids[0, 0], down_ids[0, 0]
    exps = (gate_exps[0, 0], up_exps[0, 0], down_exps[0, 0])
    values = (gate_values[0, 0], up_values[0, 0], down_values[0, 0])
    paired = (n_row, n_col) == (4, 8)
    if paired:
        tokens_all, grads_all = gather_rows(tokens, out_grad, n_row)
    else:
        tokens_all = lax.all_gather(tokens, "row", axis=0, tiled=True)
        grads_all = lax.all_gather(out_grad, "row", axis=0, tiled=True)
    total, width = tokens_all.shape
    hidden_blocks = FF_WIN // n_row // blk
    smem = pl.BlockSpec(memory_space=SMEM)
    vmem = pl.BlockSpec(memory_space=VMEM)
    params = pltpu.CompilerParams(vmem_limit_bytes=60 * 1024 * 1024)
    if paired:
        n_a = hidden_blocks * 17 // 28
        half = (n_a, 3, total // 2, blk)
        partial_shape = (
            jax.ShapeDtypeStruct(half, jnp.bfloat16),
            jax.ShapeDtypeStruct(half, jnp.float32),
            jax.ShapeDtypeStruct((hidden_blocks - n_a, 3, total, blk), jnp.float32),
        )
    else:
        partial_shape = (jax.ShapeDtypeStruct((hidden_blocks, 3, total, blk), jnp.bfloat16),)
    partial = pl.pallas_call(
        partial_kernel,
        out_shape=partial_shape,
        in_specs=[smem] * 5 + [vmem] * 5,
        out_specs=(vmem,) * len(partial_shape),
        scratch_shapes=[pltpu.VMEM((hidden_blocks, 3, total, blk), jnp.float32)],
        compiler_params=params,
        name="partial_sums",
    )(pair_slots, down_slots, *exps, tokens_all, grads_all, *values)
    acts = exchange(*partial, n_col) if paired else exchange_xla(partial[0])
    grad_shape = jax.ShapeDtypeStruct((slots, blk, blk), jnp.bfloat16)
    parts, gate_grad, up_grad, down_grad = pl.pallas_call(
        finish_kernel,
        out_shape=(jax.ShapeDtypeStruct((2, total, width), jnp.float32), grad_shape, grad_shape, grad_shape),
        in_specs=[smem] * 5 + [vmem] * 6,
        out_specs=(vmem,) * 4,
        compiler_params=params,
        name="finish",
    )(pair_slots, down_slots, *exps, tokens_all, grads_all, *values, acts)
    if paired:
        rows = sum_rows(parts, n_row)
    else:
        rows = lax.psum_scatter(parts, "row", scatter_dimension=1, tiled=True).astype(jnp.bfloat16)
    return rows[0], rows[1], gate_grad[None, None], up_grad[None, None], down_grad[None, None]


def solution(mesh):
    lists = P("row", "col", None, None, None)
    ids = P("row", "col", None)
    in_specs = (P("row", "col"), P("row", "col"), lists, ids, lists, ids, ids, lists, ids, ids)
    out_specs = (P("row", "col"), P("row", "col"), lists, lists, lists)
    body = functools.partial(on_device, mesh.shape["row"], mesh.shape["col"])
    return jax.shard_map(body, mesh=mesh, in_specs=in_specs, out_specs=out_specs, check_vma=False)
```

```python
import functools

import jax
import jax.numpy as jnp
from jax import lax
from jax.experimental import pallas as pl
from jax.experimental.pallas import tpu as pltpu
from jax.sharding import PartitionSpec as P

FF_WIN = 28672
VMEM = pltpu.VMEM
SMEM = pltpu.SMEM


def scale_of(exponent):
    return jnp.where(exponent < 0, 0.5, jnp.where(exponent > 0, 2.0, 1.0)).astype(jnp.float32)


def scaled_block(values_ref, exps_ref, slot):
    scaled = values_ref[slot].astype(jnp.float32) * scale_of(exps_ref[slot])
    return scaled.astype(jnp.bfloat16)


def dot_nt(left, right):
    return lax.dot_general(left, right, (((1,), (1,)), ((), ())), preferred_element_type=jnp.float32)


def dot_nn(left, right):
    return lax.dot_general(left, right, (((1,), (0,)), ((), ())), preferred_element_type=jnp.float32)


def dot_tn(left, right):
    return lax.dot_general(left, right, (((0,), (0,)), ((), ())), preferred_element_type=jnp.float32)


def partial_kernel(
    pair_ids, down_ids, gate_exps, up_exps, down_exps,
    tokens, grads, gate_values, up_values, down_values,
    *rest,
):
    acc = rest[-1]
    slots, blk = gate_values.shape[0], gate_values.shape[1]
    width_blocks = tokens.shape[1] // blk
    hidden_blocks = acc.shape[0]
    count = hidden_blocks * width_blocks

    @pl.loop(0, hidden_blocks)
    def _(i):
        acc[i] = jnp.zeros(acc.shape[1:], jnp.float32)

    @pl.loop(0, slots)
    def _(s):
        pair = pair_ids[s]
        down = down_ids[s]

        @pl.when(pair < count)
        def _():
            i = pair // width_blocks
            j = pair % width_blocks
            cols = tokens[:, pl.ds(pl.multiple_of(j * blk, blk), blk)]
            weights = jnp.concatenate(
                [scaled_block(gate_values, gate_exps, s), scaled_block(up_values, up_exps, s)], axis=0
            )
            both = dot_nt(cols, weights)
            acc[i, 0] += both[:, :blk]
            acc[i, 1] += both[:, blk:]

        @pl.when(down < count)
        def _():
            i = down // hidden_blocks
            j = down % hidden_blocks
            cols = grads[:, pl.ds(pl.multiple_of(i * blk, blk), blk)]
            acc[j, 2] += dot_nn(cols, scaled_block(down_values, down_exps, s))

    if len(rest) == 2:
        @pl.loop(0, hidden_blocks)
        def _(i):
            rest[0][i] = acc[i].astype(rest[0].dtype)
    else:
        sent, own, full, rounded, sems = rest[:5]
        paired, half = own.shape[0], own.shape[2]
        x = lax.axis_index("col") % 2
        mine = pl.ds(pl.multiple_of(x * half, half), half)
        theirs = pl.ds(pl.multiple_of((1 - x) * half, half), half)
        full_copy = pltpu.make_async_copy(acc.at[pl.ds(paired, hidden_blocks - paired)], full, sems.at[0])
        own_copy = pltpu.make_async_copy(acc.at[pl.ds(0, paired), :, mine], own, sems.at[1])
        full_copy.start()
        own_copy.start()

        @pl.loop(0, paired)
        def _(i):
            rounded[i] = acc[i, :, theirs].astype(rounded.dtype)

        sent_copy = pltpu.make_async_copy(rounded, sent, sems.at[2])
        sent_copy.start()
        full_copy.wait()
        own_copy.wait()
        sent_copy.wait()


def finish_kernel(
    pair_ids, down_ids, gate_exps, up_exps, down_exps,
    tokens, grads, gate_values, up_values, down_values, acts,
    parts, gate_grad, up_grad, down_grad,
):
    slots, blk = gate_values.shape[0], gate_values.shape[1]
    width_blocks = tokens.shape[1] // blk
    hidden_blocks = acts.shape[0]
    count = hidden_blocks * width_blocks

    parts[...] = jnp.zeros_like(parts)

    @pl.loop(0, slots)
    def _(s):
        pair = pair_ids[s]
        down = down_ids[s]

        @pl.when(pair < count)
        def _():
            i = pair // width_blocks
            j = pair % width_blocks
            at = pl.ds(pl.multiple_of(j * blk, blk), blk)
            cols = tokens[:, at]
            acts_both = jnp.concatenate([acts[i, 1], acts[i, 2]], axis=1)
            weights = jnp.concatenate(
                [scaled_block(gate_values, gate_exps, s), scaled_block(up_values, up_exps, s)], axis=0
            )
            parts[1, :, at] += dot_nn(acts_both, weights)
            both = dot_tn(acts_both, cols)
            gate_grad[s] = (both[:blk] * scale_of(gate_exps[s])).astype(jnp.bfloat16)
            up_grad[s] = (both[blk:] * scale_of(up_exps[s])).astype(jnp.bfloat16)

        @pl.when(pair >= count)
        def _():
            gate_grad[s] = jnp.zeros((blk, blk), jnp.bfloat16)
            up_grad[s] = jnp.zeros((blk, blk), jnp.bfloat16)

        @pl.when(down < count)
        def _():
            i = down // hidden_blocks
            j = down % hidden_blocks
            at = pl.ds(pl.multiple_of(i * blk, blk), blk)
            hidden = acts[j, 0]
            parts[0, :, at] += dot_nt(hidden, scaled_block(down_values, down_exps, s))
            grad = dot_tn(grads[:, at], hidden)
            down_grad[s] = (grad * scale_of(down_exps[s])).astype(jnp.bfloat16)

        @pl.when(down >= count)
        def _():
            down_grad[s] = jnp.zeros((blk, blk), jnp.bfloat16)


def derive(gate_sum, up_sum, hidden_grad):
    sigmoid_gate = jax.nn.sigmoid(gate_sum)
    silu = gate_sum * sigmoid_gate
    hidden = silu * up_sum
    gate_piece = hidden_grad * up_sum * sigmoid_gate * (1.0 + gate_sum * (1.0 - sigmoid_gate))
    up_piece = hidden_grad * silu
    return hidden, gate_piece, up_piece


def exchange_xla(partial):
    summed = lax.psum_scatter(partial, "col", scatter_dimension=2, tiled=True).astype(jnp.float32)
    acts = jnp.stack(derive(summed[:, 0], summed[:, 1], summed[:, 2]), axis=1).astype(jnp.bfloat16)
    return lax.all_gather(acts, "col", axis=2, tiled=True)


def activations(sums):
    return [part.astype(jnp.bfloat16) for part in derive(*sums)]


def exchange_kernel(
    n_z, ahead,
    sent, own_in, full_in, acts,
    own, from_x, from_left, from_right, to_left, to_right, stage,
    full, in_left, in_right, chain, pair_out, pair_in, joined,
    load_sem, a_send, a_recv, b_send, b_recv, pair_send, pair_recv, keep_sem, out_sem,
):
    col = lax.axis_index("col")
    z, x = col // 2, col % 2
    peer, right, left = z * 2 + (1 - x), col + 2, col - 2
    last = n_z - 1
    hop = 2
    lag = hop * last
    half = own.shape[2]
    quarter = full.shape[2] // n_z
    n_a, n_b = own.shape[0], full.shape[0]
    mine = pl.ds(pl.multiple_of(x * half, half), half)
    my_quarter = pl.ds(pl.multiple_of(z * quarter, quarter), quarter)

    def rows(d):
        return pl.ds(d * quarter, quarter)

    def remote(src, dst, send, recv, target):
        return pltpu.make_async_remote_copy(
            src_ref=src, dst_ref=dst, send_sem=send, recv_sem=recv,
            device_id={"col": target}, device_id_type=pl.DeviceIdType.MESH,
        )

    def x_copy(k):
        return remote(sent.at[k], from_x.at[k], a_send.at[0, k], a_recv.at[0, k], peer)

    def right_copy(k):
        return remote(to_right.at[k], from_left.at[k], a_send.at[1, k], a_recv.at[1, k], right)

    def left_copy(k):
        return remote(to_left.at[k], from_right.at[k], a_send.at[2, k], a_recv.at[2, k], left)

    def act_copy(k):
        return remote(stage.at[k], acts.at[k, :, mine], a_send.at[3, k], a_recv.at[3, k], peer)

    def keep_copy(k):
        return pltpu.make_async_copy(stage.at[k], acts.at[k, :, mine], keep_sem.at[k])

    def chain_right(k, d):
        return remote(chain.at[k, :, rows(d)], in_left.at[k, :, rows(d)], b_send.at[0, d, k], b_recv.at[0, d, k], right)

    def chain_left(k, d):
        return remote(chain.at[k, :, rows(d)], in_right.at[k, :, rows(d)], b_send.at[1, d, k], b_recv.at[1, d, k], left)

    def pair_copy(k):
        return remote(pair_out.at[k], pair_in.at[k], pair_send.at[k], pair_recv.at[k], peer)

    def gather_right(k, d):
        return remote(joined.at[k, :, rows(d)], joined.at[k, :, rows(d)], b_send.at[2, d, k], b_recv.at[2, d, k], right)

    def gather_left(k, d):
        return remote(joined.at[k, :, rows(d)], joined.at[k, :, rows(d)], b_send.at[3, d, k], b_recv.at[3, d, k], left)

    def out_copy(k):
        return pltpu.make_async_copy(joined.at[k], acts.at[n_a + k], out_sem.at[k])

    barrier = pltpu.get_barrier_semaphore()

    def greet(target):
        pl.semaphore_signal(barrier, inc=1, device_id={"col": target}, device_id_type=pl.DeviceIdType.MESH)

    greet(peer)
    pl.when(z > 0)(lambda: greet(left))
    pl.when(z < last)(lambda: greet(right))
    pl.semaphore_wait(barrier, 1 + (z > 0).astype(jnp.int32) + (z < last).astype(jnp.int32))

    own_load = pltpu.make_async_copy(own_in, own, load_sem.at[0])
    full_load = pltpu.make_async_copy(full_in, full, load_sem.at[1])
    for k in range(min(ahead, n_a)):
        x_copy(k).start()
    full_load.start()
    own_load.start()
    full_load.wait()
    own_load.wait()

    def f32(value):
        return value.astype(jnp.float32)

    def join(k, target, sources):
        for u in range(3):
            total = own[k, u]
            for source in sources:
                total += f32(source[k, u])
            target[k, u] = total.astype(target.dtype)

    def finish(k, sources):
        sums = []
        for u in range(3):
            total = own[k, u]
            for source in sources:
                total += f32(source[k, u])
            sums.append(total)
        for u, part in enumerate(activations(sums)):
            stage[k, u] = part

    def paired_step(t):
        @pl.when(t < n_a)
        def _():
            x_copy(t).wait_recv()
            join(t, own, [from_x])

        r = t - hop * z

        @pl.when((r >= 0) & (r < n_a) & (z < last))
        def _():
            @pl.when(z == 0)
            def _():
                join(r, to_right, [])

            @pl.when(z > 0)
            def _():
                right_copy(r).wait_recv()
                join(r, to_right, [from_left])

            right_copy(r).start()

        l = t - hop * (last - z)

        @pl.when((l >= 0) & (l < n_a) & (z > 0))
        def _():
            @pl.when(z == last)
            def _():
                join(l, to_left, [])

            @pl.when(z < last)
            def _():
                left_copy(l).wait_recv()
                join(l, to_left, [from_right])

            left_copy(l).start()

        f = t - lag

        @pl.when((f >= 0) & (f < n_a))
        def _():
            @pl.when(z == 0)
            def _():
                left_copy(f).wait_recv()
                finish(f, [from_right])

            @pl.when(z == last)
            def _():
                right_copy(f).wait_recv()
                finish(f, [from_left])

            @pl.when((z > 0) & (z < last))
            def _():
                finish(f, [from_left, from_right])

            act_copy(f).start()
            keep_copy(f).start()

    def join_rows(k, d, sources):
        for u in range(3):
            total = full[k, u, rows(d)]
            for source in sources:
                total += f32(source[k, u, rows(d)])
            chain[k, u, rows(d)] = total.astype(chain.dtype)

    def chain_step(t):
        r = t - hop * z

        @pl.when((r >= 0) & (r < n_b))
        def _():
            for d in range(1, n_z):
                @pl.when(d > z)
                def _():
                    @pl.when(z == 0)
                    def _():
                        join_rows(r, d, [])

                    @pl.when(z > 0)
                    def _():
                        chain_right(r, d).wait_recv()
                        join_rows(r, d, [in_left])

                    chain_right(r, d).start()

        l = t - hop * (last - z)

        @pl.when((l >= 0) & (l < n_b))
        def _():
            for d in range(last):
                @pl.when(d < z)
                def _():
                    @pl.when(z == last)
                    def _():
                        join_rows(l, d, [])

                    @pl.when(z < last)
                    def _():
                        chain_left(l, d).wait_recv()
                        join_rows(l, d, [in_right])

                    chain_left(l, d).start()

        f = t - lag

        @pl.when((f >= 0) & (f < n_b))
        def _():
            def add_mine(source):
                for u in range(3):
                    full[f, u, my_quarter] += f32(source[f, u, my_quarter])

            @pl.when(z > 0)
            def _():
                chain_right(f, z).wait_recv()
                add_mine(in_left)

            @pl.when(z < last)
            def _():
                chain_left(f, z).wait_recv()
                add_mine(in_right)

            pair_out[f] = full[f, :, my_quarter].astype(pair_out.dtype)
            pair_copy(f).start()

        g = t - lag - 3

        @pl.when((g >= 0) & (g < n_b))
        def _():
            pair_copy(g).wait_recv()
            sums = [full[g, u, my_quarter] + f32(pair_in[g, u]) for u in range(3)]
            for u, part in enumerate(activations(sums)):
                joined[g, u, my_quarter] = part
            pl.when(z < last)(lambda: gather_right(g, z).start())
            pl.when(z > 0)(lambda: gather_left(g, z).start())

        for d in range(n_z):
            right_at = g - hop * (z - d)
            left_at = g - hop * (d - z)

            @pl.when((d < z) & (right_at >= 0) & (right_at < n_b))
            def _():
                gather_right(right_at, d).wait_recv()
                pl.when(z < last)(lambda: gather_right(right_at, d).start())

            @pl.when((d > z) & (left_at >= 0) & (left_at < n_b))
            def _():
                gather_left(left_at, d).wait_recv()
                pl.when(z > 0)(lambda: gather_left(left_at, d).start())

        done = g - hop * last

        @pl.when((done >= 0) & (done < n_b))
        def _():
            out_copy(done).start()

    @pl.loop(0, max(n_a + lag, n_b + lag + 3 + hop * last))
    def _(t):
        first = ahead + t + (t + 1) // 2

        @pl.when(first < n_a)
        def _():
            x_copy(first).start()

        @pl.when((t % 2 == 0) & (first + 1 < n_a))
        def _():
            x_copy(first + 1).start()

        chain_step(t)
        paired_step(t)

    @pl.loop(0, n_a)
    def _(k):
        x_copy(k).wait_send()
        pl.when(z < last)(lambda: right_copy(k).wait_send())
        pl.when(z > 0)(lambda: left_copy(k).wait_send())
        act_copy(k).wait()
        keep_copy(k).wait()

    @pl.loop(0, n_b)
    def _(k):
        pair_copy(k).wait_send()
        out_copy(k).wait()
        for d in range(n_z):
            pl.when(d > z)(lambda: chain_right(k, d).wait_send())
            pl.when(d < z)(lambda: chain_left(k, d).wait_send())
            pl.when((d <= z) & (z < last))(lambda: gather_right(k, d).wait_send())
            pl.when((d >= z) & (z > 0))(lambda: gather_left(k, d).wait_send())


def exchange(sent, own, full, n_col):
    n_a, units, half, blk = own.shape
    n_b, total = full.shape[0], full.shape[2]
    n_z = n_col // 2
    bf16 = jnp.bfloat16
    halves = pltpu.VMEM((n_a, units, half, blk), bf16)
    wholes = pltpu.VMEM((n_b, units, total, blk), bf16)
    quarters = pltpu.VMEM((n_b, units, total // n_z, blk), bf16)
    dma = pltpu.SemaphoreType.DMA
    anywhere = pl.BlockSpec(memory_space=pl.ANY)
    return pl.pallas_call(
        functools.partial(exchange_kernel, n_z, min(4, n_a)),
        out_shape=jax.ShapeDtypeStruct((n_a + n_b, units, total, blk), bf16),
        in_specs=[anywhere] * 3,
        out_specs=anywhere,
        scratch_shapes=[pltpu.VMEM(own.shape, jnp.float32)] + [halves] * 6
        + [pltpu.VMEM(full.shape, jnp.float32)] + [wholes] * 3 + [quarters] * 2 + [wholes]
        + [dma((2,)), dma((4, n_a)), dma((4, n_a)), dma((4, n_z, n_b)), dma((4, n_z, n_b))]
        + [dma((n_b,)), dma((n_b,)), dma((n_a,)), dma((n_b,))],
        compiler_params=pltpu.CompilerParams(
            collective_id=0, has_side_effects=True, vmem_limit_bytes=60 * 1024 * 1024
        ),
        name="exchange",
    )(sent, own, full)


def row_neighbours():
    row = lax.axis_index("row")
    y, core = row // 2, row % 2
    return row, y, core, (1 - y) * 2 + core, y * 2 + (1 - core)


def row_remote(src, dst, send, recv, target):
    return pltpu.make_async_remote_copy(
        src_ref=src, dst_ref=dst, send_sem=send, recv_sem=recv,
        device_id={"row": target}, device_id_type=pl.DeviceIdType.MESH,
    )


def row_barrier(targets):
    barrier = pltpu.get_barrier_semaphore()
    for target in targets:
        pl.semaphore_signal(barrier, inc=1, device_id={"row": target}, device_id_type=pl.DeviceIdType.MESH)
    pl.semaphore_wait(barrier, len(targets))


def gather_kernel(tokens, grads, tokens_all, grads_all, send, recv, keep):
    row, y, core, far, near = row_neighbours()
    share = tokens.shape[0]
    row_barrier((far, near))

    def rows(index):
        return pl.ds(pl.multiple_of(index * share, share), share)

    pairs = ((tokens, tokens_all), (grads, grads_all))
    across = [row_remote(src, dst.at[rows(row)], send.at[0, a], recv.at[0, a], far) for a, (src, dst) in enumerate(pairs)]
    beside = [row_remote(src, dst.at[rows(row)], send.at[1, a], recv.at[1, a], near) for a, (src, dst) in enumerate(pairs)]
    onward = [
        row_remote(dst.at[rows(far)], dst.at[rows(far)], send.at[2, a], recv.at[2, a], near)
        for a, (src, dst) in enumerate(pairs)
    ]
    local = [pltpu.make_async_copy(src, dst.at[rows(row)], keep.at[a]) for a, (src, dst) in enumerate(pairs)]
    for copy in across + beside + local:
        copy.start()
    for a in range(2):
        across[a].wait_recv()
        onward[a].start()
    for a in range(2):
        across[a].wait_send()
        beside[a].wait()
        onward[a].wait()
        local[a].wait()


def gather_rows(tokens, grads, n_row):
    whole = jax.ShapeDtypeStruct((tokens.shape[0] * n_row, tokens.shape[1]), tokens.dtype)
    anywhere = pl.BlockSpec(memory_space=pl.ANY)
    dma = pltpu.SemaphoreType.DMA
    return pl.pallas_call(
        gather_kernel,
        out_shape=(whole, whole),
        in_specs=[anywhere] * 2,
        out_specs=(anywhere,) * 2,
        scratch_shapes=[dma((3, 2)), dma((3, 2)), dma((2,))],
        compiler_params=pltpu.CompilerParams(collective_id=1, has_side_effects=True),
        name="gather_rows",
    )(tokens, grads)


def sum_kernel(parts, output, input_grad, from_near, to_far, from_far, send, recv):
    row, y, core, far, near = row_neighbours()
    share = output.shape[0]
    results = (output, input_grad)
    row_barrier((far, near))

    def rows(index):
        return pl.ds(pl.multiple_of(index * share, share), share)

    def near_copy(place, u):
        index = jnp.where(place == 0, 1 - y, y) * 2 + (1 - core)
        return row_remote(
            parts.at[u, rows(index)], from_near.at[place, u], send.at[place, u], recv.at[place, u], near
        )

    def far_copy(u):
        return row_remote(to_far.at[u], from_far.at[u], send.at[2, u], recv.at[2, u], far)

    for place in range(2):
        for u in range(2):
            near_copy(place, u).start()
    for u in range(2):
        near_copy(0, u).wait_recv()
        to_far[u] = (parts[u, rows(far)] + from_near[0, u]).astype(to_far.dtype)
        far_copy(u).start()
    for u in range(2):
        near_copy(1, u).wait_recv()
        from_near[1, u] += parts[u, rows(row)]
    for u in range(2):
        far_copy(u).wait_recv()
        results[u][...] = (from_near[1, u] + from_far[u].astype(jnp.float32)).astype(jnp.bfloat16)
    for u in range(2):
        near_copy(0, u).wait_send()
        near_copy(1, u).wait_send()
        far_copy(u).wait_send()


def sum_rows(parts, n_row):
    units, total, width = parts.shape
    share = total // n_row
    result = jax.ShapeDtypeStruct((share, width), jnp.bfloat16)
    vmem = pl.BlockSpec(memory_space=VMEM)
    dma = pltpu.SemaphoreType.DMA
    return pl.pallas_call(
        sum_kernel,
        out_shape=(result, result),
        in_specs=[vmem],
        out_specs=(vmem, vmem),
        scratch_shapes=[
            pltpu.VMEM((2, units, share, width), jnp.float32),
            pltpu.VMEM((units, share, width), jnp.bfloat16),
            pltpu.VMEM((units, share, width), jnp.bfloat16),
            dma((3, units)), dma((3, units)),
        ],
        compiler_params=pltpu.CompilerParams(
            collective_id=2, has_side_effects=True, vmem_limit_bytes=32 * 1024 * 1024
        ),
        name="sum_rows",
    )(parts)


def on_device(
    n_row, n_col,
    tokens, out_grad, gate_values, gate_exps, up_values, up_exps, gate_up_ids,
    down_values, down_exps, down_ids,
):
    blk = gate_values.shape[-1]
    slots = gate_values.shape[2]
    pair_slots, down_slots = gate_up_ids[0, 0], down_ids[0, 0]
    exps = (gate_exps[0, 0], up_exps[0, 0], down_exps[0, 0])
    values = (gate_values[0, 0], up_values[0, 0], down_values[0, 0])
    paired = (n_row, n_col) == (4, 8)
    if paired:
        tokens_all, grads_all = gather_rows(tokens, out_grad, n_row)
    else:
        tokens_all = lax.all_gather(tokens, "row", axis=0, tiled=True)
        grads_all = lax.all_gather(out_grad, "row", axis=0, tiled=True)
    total, width = tokens_all.shape
    hidden_blocks = FF_WIN // n_row // blk
    smem = pl.BlockSpec(memory_space=SMEM)
    vmem = pl.BlockSpec(memory_space=VMEM)
    params = pltpu.CompilerParams(vmem_limit_bytes=60 * 1024 * 1024)
    if paired:
        n_a = hidden_blocks * 17 // 28
        half = (n_a, 3, total // 2, blk)
        partial_shape = (
            jax.ShapeDtypeStruct(half, jnp.bfloat16),
            jax.ShapeDtypeStruct(half, jnp.float32),
            jax.ShapeDtypeStruct((hidden_blocks - n_a, 3, total, blk), jnp.float32),
        )
        partial_scratch = [pltpu.VMEM(half, jnp.bfloat16), pltpu.SemaphoreType.DMA((3,))]
    else:
        partial_shape = (jax.ShapeDtypeStruct((hidden_blocks, 3, total, blk), jnp.bfloat16),)
        partial_scratch = []
    partial = pl.pallas_call(
        partial_kernel,
        out_shape=partial_shape,
        in_specs=[smem] * 5 + [vmem] * 5,
        out_specs=(pl.BlockSpec(memory_space=pl.ANY) if paired else vmem,) * len(partial_shape),
        scratch_shapes=partial_scratch + [pltpu.VMEM((hidden_blocks, 3, total, blk), jnp.float32)],
        compiler_params=params,
        name="partial_sums",
    )(pair_slots, down_slots, *exps, tokens_all, grads_all, *values)
    acts = exchange(*partial, n_col) if paired else exchange_xla(partial[0])
    grad_shape = jax.ShapeDtypeStruct((slots, blk, blk), jnp.bfloat16)
    parts, gate_grad, up_grad, down_grad = pl.pallas_call(
        finish_kernel,
        out_shape=(jax.ShapeDtypeStruct((2, total, width), jnp.float32), grad_shape, grad_shape, grad_shape),
        in_specs=[smem] * 5 + [vmem] * 6,
        out_specs=(vmem,) * 4,
        compiler_params=params,
        name="finish",
    )(pair_slots, down_slots, *exps, tokens_all, grads_all, *values, acts)
    if paired:
        rows = sum_rows(parts, n_row)
    else:
        rows = lax.psum_scatter(parts, "row", scatter_dimension=1, tiled=True).astype(jnp.bfloat16)
    return rows[0], rows[1], gate_grad[None, None], up_grad[None, None], down_grad[None, None]


def solution(mesh):
    lists = P("row", "col", None, None, None)
    ids = P("row", "col", None)
    in_specs = (P("row", "col"), P("row", "col"), lists, ids, lists, ids, ids, lists, ids, ids)
    out_specs = (P("row", "col"), P("row", "col"), lists, lists, lists)
    body = functools.partial(on_device, mesh.shape["row"], mesh.shape["col"])
    return jax.shard_map(body, mesh=mesh, in_specs=in_specs, out_specs=out_specs, check_vma=False)
```

```python
import functools

import jax
import jax.numpy as jnp
from jax import lax
from jax.experimental import pallas as pl
from jax.experimental.pallas import tpu as pltpu
from jax.sharding import PartitionSpec as P

FF_WIN = 28672
VMEM = pltpu.VMEM
SMEM = pltpu.SMEM


def scale_of(exponent):
    return jnp.where(exponent < 0, 0.5, jnp.where(exponent > 0, 2.0, 1.0)).astype(jnp.float32)


def scaled_block(values_ref, exps_ref, slot):
    scaled = values_ref[slot].astype(jnp.float32) * scale_of(exps_ref[slot])
    return scaled.astype(jnp.bfloat16)


def dot_nt(left, right):
    return lax.dot_general(left, right, (((1,), (1,)), ((), ())), preferred_element_type=jnp.float32)


def dot_nn(left, right):
    return lax.dot_general(left, right, (((1,), (0,)), ((), ())), preferred_element_type=jnp.float32)


def dot_tn(left, right):
    return lax.dot_general(left, right, (((0,), (0,)), ((), ())), preferred_element_type=jnp.float32)


def partial_kernel(
    pair_ids, down_ids, gate_exps, up_exps, down_exps,
    tokens_in, grads_in, gate_in, up_in, down_in,
    *rest,
):
    tokens, grads, gate_values, up_values, down_values, load_sem, acc = rest[-7:]
    rest = rest[:-6]
    operands = (tokens_in, grads_in, gate_in, up_in, down_in)
    places = (tokens, grads, gate_values, up_values, down_values)
    loads = [pltpu.make_async_copy(src, dst, load_sem.at[n]) for n, (src, dst) in enumerate(zip(operands, places))]
    for load in loads:
        load.start()
    slots, blk = gate_values.shape[0], gate_values.shape[1]
    width_blocks = tokens.shape[1] // blk
    hidden_blocks = acc.shape[0]
    count = hidden_blocks * width_blocks

    @pl.loop(0, hidden_blocks)
    def _(i):
        acc[i] = jnp.zeros(acc.shape[1:], jnp.float32)

    for load in loads:
        load.wait()

    @pl.loop(0, slots)
    def _(s):
        pair = pair_ids[s]
        down = down_ids[s]

        @pl.when(pair < count)
        def _():
            i = pair // width_blocks
            j = pair % width_blocks
            cols = tokens[:, pl.ds(pl.multiple_of(j * blk, blk), blk)]
            weights = jnp.concatenate(
                [scaled_block(gate_values, gate_exps, s), scaled_block(up_values, up_exps, s)], axis=0
            )
            both = dot_nt(cols, weights)
            acc[i, 0] += both[:, :blk]
            acc[i, 1] += both[:, blk:]

        @pl.when(down < count)
        def _():
            i = down // hidden_blocks
            j = down % hidden_blocks
            cols = grads[:, pl.ds(pl.multiple_of(i * blk, blk), blk)]
            acc[j, 2] += dot_nn(cols, scaled_block(down_values, down_exps, s))

    if len(rest) == 2:
        @pl.loop(0, hidden_blocks)
        def _(i):
            rest[0][i] = acc[i].astype(rest[0].dtype)
    else:
        sent, own, full, rounded, sems = rest[:5]
        paired, half = own.shape[0], own.shape[2]
        x = lax.axis_index("col") % 2
        mine = pl.ds(pl.multiple_of(x * half, half), half)
        theirs = pl.ds(pl.multiple_of((1 - x) * half, half), half)
        full_copy = pltpu.make_async_copy(acc.at[pl.ds(paired, hidden_blocks - paired)], full, sems.at[0])
        own_copy = pltpu.make_async_copy(acc.at[pl.ds(0, paired), :, mine], own, sems.at[1])
        full_copy.start()
        own_copy.start()

        @pl.loop(0, paired)
        def _(i):
            rounded[i] = acc[i, :, theirs].astype(rounded.dtype)

        sent_copy = pltpu.make_async_copy(rounded, sent, sems.at[2])
        sent_copy.start()
        full_copy.wait()
        own_copy.wait()
        sent_copy.wait()


def finish_kernel(
    pair_ids, down_ids, gate_exps, up_exps, down_exps,
    tokens, grads, gate_values, up_values, down_values, acts,
    parts, gate_grad, up_grad, down_grad,
):
    slots, blk = gate_values.shape[0], gate_values.shape[1]
    width_blocks = tokens.shape[1] // blk
    hidden_blocks = acts.shape[0]
    count = hidden_blocks * width_blocks

    parts[...] = jnp.zeros_like(parts)

    @pl.loop(0, slots)
    def _(s):
        pair = pair_ids[s]
        down = down_ids[s]

        @pl.when(pair < count)
        def _():
            i = pair // width_blocks
            j = pair % width_blocks
            at = pl.ds(pl.multiple_of(j * blk, blk), blk)
            cols = tokens[:, at]
            acts_both = jnp.concatenate([acts[i, 1], acts[i, 2]], axis=1)
            weights = jnp.concatenate(
                [scaled_block(gate_values, gate_exps, s), scaled_block(up_values, up_exps, s)], axis=0
            )
            parts[1, :, at] += dot_nn(acts_both, weights)
            both = dot_tn(acts_both, cols)
            gate_grad[s] = (both[:blk] * scale_of(gate_exps[s])).astype(jnp.bfloat16)
            up_grad[s] = (both[blk:] * scale_of(up_exps[s])).astype(jnp.bfloat16)

        @pl.when(pair >= count)
        def _():
            gate_grad[s] = jnp.zeros((blk, blk), jnp.bfloat16)
            up_grad[s] = jnp.zeros((blk, blk), jnp.bfloat16)

        @pl.when(down < count)
        def _():
            i = down // hidden_blocks
            j = down % hidden_blocks
            at = pl.ds(pl.multiple_of(i * blk, blk), blk)
            hidden = acts[j, 0]
            parts[0, :, at] += dot_nt(hidden, scaled_block(down_values, down_exps, s))
            grad = dot_tn(grads[:, at], hidden)
            down_grad[s] = (grad * scale_of(down_exps[s])).astype(jnp.bfloat16)

        @pl.when(down >= count)
        def _():
            down_grad[s] = jnp.zeros((blk, blk), jnp.bfloat16)


def derive(gate_sum, up_sum, hidden_grad):
    sigmoid_gate = jax.nn.sigmoid(gate_sum)
    silu = gate_sum * sigmoid_gate
    hidden = silu * up_sum
    gate_piece = hidden_grad * up_sum * sigmoid_gate * (1.0 + gate_sum * (1.0 - sigmoid_gate))
    up_piece = hidden_grad * silu
    return hidden, gate_piece, up_piece


def exchange_xla(partial):
    summed = lax.psum_scatter(partial, "col", scatter_dimension=2, tiled=True).astype(jnp.float32)
    acts = jnp.stack(derive(summed[:, 0], summed[:, 1], summed[:, 2]), axis=1).astype(jnp.bfloat16)
    return lax.all_gather(acts, "col", axis=2, tiled=True)


def activations(sums):
    return [part.astype(jnp.bfloat16) for part in derive(*sums)]


def exchange_kernel(
    n_z, ahead,
    sent, own_in, full_in, acts,
    own, from_x, from_left, from_right, to_left, to_right, stage,
    full, in_left, in_right, chain, pair_out, pair_in, joined,
    load_sem, a_send, a_recv, b_send, b_recv, pair_send, pair_recv, keep_sem, out_sem,
):
    col = lax.axis_index("col")
    z, x = col // 2, col % 2
    peer, right, left = z * 2 + (1 - x), col + 2, col - 2
    last = n_z - 1
    hop, b_hop = 2, 1
    lag, b_lag = hop * last, b_hop * last + 1
    half = own.shape[2]
    quarter = full.shape[2] // n_z
    n_a, n_b = own.shape[0], full.shape[0]
    mine = pl.ds(pl.multiple_of(x * half, half), half)
    my_quarter = pl.ds(pl.multiple_of(z * quarter, quarter), quarter)

    def rows(d):
        return pl.ds(d * quarter, quarter)

    def remote(src, dst, send, recv, target):
        return pltpu.make_async_remote_copy(
            src_ref=src, dst_ref=dst, send_sem=send, recv_sem=recv,
            device_id={"col": target}, device_id_type=pl.DeviceIdType.MESH,
        )

    def x_copy(k):
        return remote(sent.at[k], from_x.at[k], a_send.at[0, k], a_recv.at[0, k], peer)

    def right_copy(k):
        return remote(to_right.at[k], from_left.at[k], a_send.at[1, k], a_recv.at[1, k], right)

    def left_copy(k):
        return remote(to_left.at[k], from_right.at[k], a_send.at[2, k], a_recv.at[2, k], left)

    def act_copy(k):
        return remote(stage.at[k], acts.at[k, :, mine], a_send.at[3, k], a_recv.at[3, k], peer)

    def keep_copy(k):
        return pltpu.make_async_copy(stage.at[k], acts.at[k, :, mine], keep_sem.at[k])

    def chain_right(k, d):
        return remote(chain.at[k, :, rows(d)], in_left.at[k, :, rows(d)], b_send.at[0, d, k], b_recv.at[0, d, k], right)

    def chain_left(k, d):
        return remote(chain.at[k, :, rows(d)], in_right.at[k, :, rows(d)], b_send.at[1, d, k], b_recv.at[1, d, k], left)

    def pair_copy(k):
        return remote(pair_out.at[k], pair_in.at[k], pair_send.at[k], pair_recv.at[k], peer)

    def gather_right(k, d):
        return remote(joined.at[k, :, rows(d)], joined.at[k, :, rows(d)], b_send.at[2, d, k], b_recv.at[2, d, k], right)

    def gather_left(k, d):
        return remote(joined.at[k, :, rows(d)], joined.at[k, :, rows(d)], b_send.at[3, d, k], b_recv.at[3, d, k], left)

    def out_copy(k):
        return pltpu.make_async_copy(joined.at[k], acts.at[n_a + k], out_sem.at[k])

    barrier = pltpu.get_barrier_semaphore()

    def greet(target):
        pl.semaphore_signal(barrier, inc=1, device_id={"col": target}, device_id_type=pl.DeviceIdType.MESH)

    greet(peer)
    pl.when(z > 0)(lambda: greet(left))
    pl.when(z < last)(lambda: greet(right))
    pl.semaphore_wait(barrier, 1 + (z > 0).astype(jnp.int32) + (z < last).astype(jnp.int32))

    own_load = pltpu.make_async_copy(own_in, own, load_sem.at[0])
    full_load = pltpu.make_async_copy(full_in, full, load_sem.at[1])
    for k in range(min(ahead, n_a)):
        x_copy(k).start()
    full_load.start()
    own_load.start()
    full_load.wait()

    def f32(value):
        return value.astype(jnp.float32)

    def join(k, target, sources):
        for u in range(3):
            total = own[k, u]
            for source in sources:
                total += f32(source[k, u])
            target[k, u] = total.astype(target.dtype)

    def finish(k, sources):
        sums = []
        for u in range(3):
            total = own[k, u]
            for source in sources:
                total += f32(source[k, u])
            sums.append(total)
        for u, part in enumerate(activations(sums)):
            stage[k, u] = part

    def paired_step(t):
        @pl.when(t < n_a)
        def _():
            x_copy(t).wait_recv()
            join(t, own, [from_x])

        r = t - hop * z

        @pl.when((r >= 0) & (r < n_a) & (z < last))
        def _():
            @pl.when(z == 0)
            def _():
                join(r, to_right, [])

            @pl.when(z > 0)
            def _():
                right_copy(r).wait_recv()
                join(r, to_right, [from_left])

            right_copy(r).start()

        l = t - hop * (last - z)

        @pl.when((l >= 0) & (l < n_a) & (z > 0))
        def _():
            @pl.when(z == last)
            def _():
                join(l, to_left, [])

            @pl.when(z < last)
            def _():
                left_copy(l).wait_recv()
                join(l, to_left, [from_right])

            left_copy(l).start()

        f = t - lag

        @pl.when((f >= 0) & (f < n_a))
        def _():
            @pl.when(z == 0)
            def _():
                left_copy(f).wait_recv()
                finish(f, [from_right])

            @pl.when(z == last)
            def _():
                right_copy(f).wait_recv()
                finish(f, [from_left])

            @pl.when((z > 0) & (z < last))
            def _():
                finish(f, [from_left, from_right])

            act_copy(f).start()
            keep_copy(f).start()

    def join_rows(k, d, sources):
        for u in range(3):
            total = full[k, u, rows(d)]
            for source in sources:
                total += f32(source[k, u, rows(d)])
            chain[k, u, rows(d)] = total.astype(chain.dtype)

    def chain_step(t):
        r = t - b_hop * z

        @pl.when((r >= 0) & (r < n_b))
        def _():
            for d in range(1, n_z):
                @pl.when(d > z)
                def _():
                    @pl.when(z == 0)
                    def _():
                        join_rows(r, d, [])

                    @pl.when(z > 0)
                    def _():
                        chain_right(r, d).wait_recv()
                        join_rows(r, d, [in_left])

                    chain_right(r, d).start()

        l = t - b_hop * (last - z)

        @pl.when((l >= 0) & (l < n_b))
        def _():
            for d in range(last):
                @pl.when(d < z)
                def _():
                    @pl.when(z == last)
                    def _():
                        join_rows(l, d, [])

                    @pl.when(z < last)
                    def _():
                        chain_left(l, d).wait_recv()
                        join_rows(l, d, [in_right])

                    chain_left(l, d).start()

        f = t - b_lag

        @pl.when((f >= 0) & (f < n_b))
        def _():
            def add_mine(source):
                for u in range(3):
                    full[f, u, my_quarter] += f32(source[f, u, my_quarter])

            @pl.when(z > 0)
            def _():
                chain_right(f, z).wait_recv()
                add_mine(in_left)

            @pl.when(z < last)
            def _():
                chain_left(f, z).wait_recv()
                add_mine(in_right)

            pair_out[f] = full[f, :, my_quarter].astype(pair_out.dtype)
            pair_copy(f).start()

        g = t - b_lag - 2

        @pl.when((g >= 0) & (g < n_b))
        def _():
            pair_copy(g).wait_recv()
            sums = [full[g, u, my_quarter] + f32(pair_in[g, u]) for u in range(3)]
            for u, part in enumerate(activations(sums)):
                joined[g, u, my_quarter] = part
            pl.when(z < last)(lambda: gather_right(g, z).start())
            pl.when(z > 0)(lambda: gather_left(g, z).start())

        for d in range(n_z):
            right_at = g - b_hop * (z - d)
            left_at = g - b_hop * (d - z)

            @pl.when((d < z) & (right_at >= 0) & (right_at < n_b))
            def _():
                gather_right(right_at, d).wait_recv()
                pl.when(z < last)(lambda: gather_right(right_at, d).start())

            @pl.when((d > z) & (left_at >= 0) & (left_at < n_b))
            def _():
                gather_left(left_at, d).wait_recv()
                pl.when(z > 0)(lambda: gather_left(left_at, d).start())

        done = g - b_hop * last

        @pl.when((done >= 0) & (done < n_b))
        def _():
            out_copy(done).start()

    @pl.loop(0, max(n_a + lag, n_b + b_lag + 2 + b_hop * last))
    def _(t):
        first = ahead + t + (t + 1) // 2

        @pl.when(first < n_a)
        def _():
            x_copy(first).start()

        @pl.when((t % 2 == 0) & (first + 1 < n_a))
        def _():
            x_copy(first + 1).start()

        chain_step(t)
        pl.when(t == 0)(lambda: own_load.wait())
        paired_step(t)

    @pl.loop(0, n_a)
    def _(k):
        x_copy(k).wait_send()
        pl.when(z < last)(lambda: right_copy(k).wait_send())
        pl.when(z > 0)(lambda: left_copy(k).wait_send())
        act_copy(k).wait()
        keep_copy(k).wait()

    @pl.loop(0, n_b)
    def _(k):
        pair_copy(k).wait_send()
        out_copy(k).wait()
        for d in range(n_z):
            pl.when(d > z)(lambda: chain_right(k, d).wait_send())
            pl.when(d < z)(lambda: chain_left(k, d).wait_send())
            pl.when((d <= z) & (z < last))(lambda: gather_right(k, d).wait_send())
            pl.when((d >= z) & (z > 0))(lambda: gather_left(k, d).wait_send())


def exchange(sent, own, full, n_col):
    n_a, units, half, blk = own.shape
    n_b, total = full.shape[0], full.shape[2]
    n_z = n_col // 2
    bf16 = jnp.bfloat16
    halves = pltpu.VMEM((n_a, units, half, blk), bf16)
    wholes = pltpu.VMEM((n_b, units, total, blk), bf16)
    quarters = pltpu.VMEM((n_b, units, total // n_z, blk), bf16)
    dma = pltpu.SemaphoreType.DMA
    anywhere = pl.BlockSpec(memory_space=pl.ANY)
    return pl.pallas_call(
        functools.partial(exchange_kernel, n_z, min(4, n_a)),
        out_shape=jax.ShapeDtypeStruct((n_a + n_b, units, total, blk), bf16),
        in_specs=[anywhere] * 3,
        out_specs=anywhere,
        scratch_shapes=[pltpu.VMEM(own.shape, jnp.float32)] + [halves] * 6
        + [pltpu.VMEM(full.shape, jnp.float32)] + [wholes] * 3 + [quarters] * 2 + [wholes]
        + [dma((2,)), dma((4, n_a)), dma((4, n_a)), dma((4, n_z, n_b)), dma((4, n_z, n_b))]
        + [dma((n_b,)), dma((n_b,)), dma((n_a,)), dma((n_b,))],
        compiler_params=pltpu.CompilerParams(
            collective_id=0, has_side_effects=True, vmem_limit_bytes=60 * 1024 * 1024
        ),
        name="exchange",
    )(sent, own, full)


def row_neighbours():
    row = lax.axis_index("row")
    y, core = row // 2, row % 2
    return row, y, core, (1 - y) * 2 + core, y * 2 + (1 - core)


def row_remote(src, dst, send, recv, target):
    return pltpu.make_async_remote_copy(
        src_ref=src, dst_ref=dst, send_sem=send, recv_sem=recv,
        device_id={"row": target}, device_id_type=pl.DeviceIdType.MESH,
    )


def row_barrier(targets):
    barrier = pltpu.get_barrier_semaphore()
    for target in targets:
        pl.semaphore_signal(barrier, inc=1, device_id={"row": target}, device_id_type=pl.DeviceIdType.MESH)
    pl.semaphore_wait(barrier, len(targets))


def gather_kernel(tokens, grads, tokens_all, grads_all, send, recv, keep):
    row, y, core, far, near = row_neighbours()
    share = tokens.shape[0]
    row_barrier((far, near))

    def rows(index):
        return pl.ds(pl.multiple_of(index * share, share), share)

    pairs = ((tokens, tokens_all), (grads, grads_all))
    across = [row_remote(src, dst.at[rows(row)], send.at[0, a], recv.at[0, a], far) for a, (src, dst) in enumerate(pairs)]
    beside = [row_remote(src, dst.at[rows(row)], send.at[1, a], recv.at[1, a], near) for a, (src, dst) in enumerate(pairs)]
    onward = [
        row_remote(dst.at[rows(far)], dst.at[rows(far)], send.at[2, a], recv.at[2, a], near)
        for a, (src, dst) in enumerate(pairs)
    ]
    local = [pltpu.make_async_copy(src, dst.at[rows(row)], keep.at[a]) for a, (src, dst) in enumerate(pairs)]
    for copy in across + beside + local:
        copy.start()
    for a in range(2):
        across[a].wait_recv()
        onward[a].start()
    for a in range(2):
        across[a].wait_send()
        beside[a].wait()
        onward[a].wait()
        local[a].wait()


def gather_rows(tokens, grads, n_row):
    whole = jax.ShapeDtypeStruct((tokens.shape[0] * n_row, tokens.shape[1]), tokens.dtype)
    anywhere = pl.BlockSpec(memory_space=pl.ANY)
    dma = pltpu.SemaphoreType.DMA
    return pl.pallas_call(
        gather_kernel,
        out_shape=(whole, whole),
        in_specs=[anywhere] * 2,
        out_specs=(anywhere,) * 2,
        scratch_shapes=[dma((3, 2)), dma((3, 2)), dma((2,))],
        compiler_params=pltpu.CompilerParams(collective_id=1, has_side_effects=True),
        name="gather_rows",
    )(tokens, grads)


def sum_kernel(parts, output, input_grad, kept, from_near, to_far, from_far, send, recv, load):
    row, y, core, far, near = row_neighbours()
    share = output.shape[0]
    results = (output, input_grad)
    row_barrier((far, near))

    def rows(index):
        return pl.ds(pl.multiple_of(index * share, share), share)

    def near_copy(place, u):
        index = jnp.where(place == 0, 1 - y, y) * 2 + (1 - core)
        return row_remote(
            parts.at[u, rows(index)], from_near.at[place, u], send.at[place, u], recv.at[place, u], near
        )

    def far_copy(u):
        return row_remote(to_far.at[u], from_far.at[u], send.at[2, u], recv.at[2, u], far)

    def load_copy(place, u):
        return pltpu.make_async_copy(parts.at[u, rows((far, row)[place])], kept.at[place, u], load.at[place, u])

    for place in range(2):
        for u in range(2):
            near_copy(place, u).start()
            load_copy(place, u).start()
    for u in range(2):
        load_copy(0, u).wait()
        near_copy(0, u).wait_recv()
        to_far[u] = (kept[0, u] + from_near[0, u]).astype(to_far.dtype)
        far_copy(u).start()
    for u in range(2):
        load_copy(1, u).wait()
        near_copy(1, u).wait_recv()
        from_near[1, u] += kept[1, u]
    for u in range(2):
        far_copy(u).wait_recv()
        results[u][...] = (from_near[1, u] + from_far[u].astype(jnp.float32)).astype(jnp.bfloat16)
    for u in range(2):
        near_copy(0, u).wait_send()
        near_copy(1, u).wait_send()
        far_copy(u).wait_send()


def sum_rows(parts, n_row):
    units, total, width = parts.shape
    share = total // n_row
    result = jax.ShapeDtypeStruct((share, width), jnp.bfloat16)
    vmem = pl.BlockSpec(memory_space=VMEM)
    dma = pltpu.SemaphoreType.DMA
    return pl.pallas_call(
        sum_kernel,
        out_shape=(result, result),
        in_specs=[pl.BlockSpec(memory_space=pl.ANY)],
        out_specs=(vmem, vmem),
        scratch_shapes=[
            pltpu.VMEM((2, units, share, width), jnp.float32),
            pltpu.VMEM((2, units, share, width), jnp.float32),
            pltpu.VMEM((units, share, width), jnp.bfloat16),
            pltpu.VMEM((units, share, width), jnp.bfloat16),
            dma((3, units)), dma((3, units)), dma((2, units)),
        ],
        compiler_params=pltpu.CompilerParams(
            collective_id=2, has_side_effects=True, vmem_limit_bytes=60 * 1024 * 1024
        ),
        name="sum_rows",
    )(parts)


def on_device(
    n_row, n_col,
    tokens, out_grad, gate_values, gate_exps, up_values, up_exps, gate_up_ids,
    down_values, down_exps, down_ids,
):
    blk = gate_values.shape[-1]
    slots = gate_values.shape[2]
    pair_slots, down_slots = gate_up_ids[0, 0], down_ids[0, 0]
    exps = (gate_exps[0, 0], up_exps[0, 0], down_exps[0, 0])
    values = (gate_values[0, 0], up_values[0, 0], down_values[0, 0])
    paired = (n_row, n_col) == (4, 8)
    if paired:
        tokens_all, grads_all = gather_rows(tokens, out_grad, n_row)
    else:
        tokens_all = lax.all_gather(tokens, "row", axis=0, tiled=True)
        grads_all = lax.all_gather(out_grad, "row", axis=0, tiled=True)
    total, width = tokens_all.shape
    hidden_blocks = FF_WIN // n_row // blk
    smem = pl.BlockSpec(memory_space=SMEM)
    vmem = pl.BlockSpec(memory_space=VMEM)
    params = pltpu.CompilerParams(vmem_limit_bytes=60 * 1024 * 1024)
    if paired:
        n_a = hidden_blocks * 9 // 14
        half = (n_a, 3, total // 2, blk)
        partial_shape = (
            jax.ShapeDtypeStruct(half, jnp.bfloat16),
            jax.ShapeDtypeStruct(half, jnp.float32),
            jax.ShapeDtypeStruct((hidden_blocks - n_a, 3, total, blk), jnp.float32),
        )
        partial_scratch = [pltpu.VMEM(half, jnp.bfloat16), pltpu.SemaphoreType.DMA((3,))]
    else:
        partial_shape = (jax.ShapeDtypeStruct((hidden_blocks, 3, total, blk), jnp.bfloat16),)
        partial_scratch = []
    partial = pl.pallas_call(
        partial_kernel,
        out_shape=partial_shape,
        in_specs=[smem] * 5 + [pl.BlockSpec(memory_space=pl.ANY)] * 5,
        out_specs=(pl.BlockSpec(memory_space=pl.ANY) if paired else vmem,) * len(partial_shape),
        scratch_shapes=partial_scratch
        + [pltpu.VMEM(each.shape, each.dtype) for each in (tokens_all, grads_all, *values)]
        + [pltpu.SemaphoreType.DMA((5,)), pltpu.VMEM((hidden_blocks, 3, total, blk), jnp.float32)],
        compiler_params=params,
        name="partial_sums",
    )(pair_slots, down_slots, *exps, tokens_all, grads_all, *values)
    acts = exchange(*partial, n_col) if paired else exchange_xla(partial[0])
    grad_shape = jax.ShapeDtypeStruct((slots, blk, blk), jnp.bfloat16)
    parts, gate_grad, up_grad, down_grad = pl.pallas_call(
        finish_kernel,
        out_shape=(jax.ShapeDtypeStruct((2, total, width), jnp.float32), grad_shape, grad_shape, grad_shape),
        in_specs=[smem] * 5 + [vmem] * 6,
        out_specs=(vmem,) * 4,
        compiler_params=params,
        name="finish",
    )(pair_slots, down_slots, *exps, tokens_all, grads_all, *values, acts)
    if paired:
        rows = sum_rows(parts, n_row)
    else:
        rows = lax.psum_scatter(parts, "row", scatter_dimension=1, tiled=True).astype(jnp.bfloat16)
    return rows[0], rows[1], gate_grad[None, None], up_grad[None, None], down_grad[None, None]


def solution(mesh):
    lists = P("row", "col", None, None, None)
    ids = P("row", "col", None)
    in_specs = (P("row", "col"), P("row", "col"), lists, ids, lists, ids, ids, lists, ids, ids)
    out_specs = (P("row", "col"), P("row", "col"), lists, lists, lists)
    body = functools.partial(on_device, mesh.shape["row"], mesh.shape["col"])
    return jax.shard_map(body, mesh=mesh, in_specs=in_specs, out_specs=out_specs, check_vma=False)
```
